32 devices in a mesh: groups: 2 (over x), tensor: 8 (over z, y), dp: 2 (over core).
Axes of the slice: x: 2, y: 2, z: 4, core: 2. Of those that a mesh axis runs over, the one named last changes fastest.
Arguments:
- hidden_act: bfloat16 [1536, 28672], P(('groups', 'dp'), 'tensor'), parts along dimension 0, may hold values from -6 to 6
- down_weight: bfloat16 [28672, 8192], P('tensor', 'dp'), may hold values from -0.046875 to 0.046875
- residual: bfloat16 [1536, 8192], P(('groups', 'dp'), 'tensor'), parts along dimension 0, may hold values from -6 to 6
- tap_early: bfloat16 [1536, 8192], P(('groups', 'dp'), 'tensor'), parts along dimension 0, may hold values from -6 to 6
- tap_middle: bfloat16 [1536, 8192], P(('groups', 'dp'), 'tensor'), parts along dimension 0, may hold values from -6 to 6
- merge_weight: bfloat16 [3, 8192, 5120], P(None, 'tensor', 'dp'), may hold values from -0.0546875 to 0.0546875
- q_gain: float32 [128], replicated, may hold values from 0.5 to 2
- k_gain: float32 [128], replicated, may hold values from 0.5 to 2
- lengths: int32 [4, 16], P(('groups', 'dp')), parts along dimension 0, may hold values from 1 to 93
- offsets: int32 [4, 16], P(('groups', 'dp')), parts along dimension 0, may hold values from 0 to 383, as said below
- owner_map: int32 [4, 16], P(('groups', 'dp')), parts along dimension 0, may hold values from 0 to 7, as said below
- loss_mask: int32 [1536], P(('groups', 'dp')), parts along dimension 0, may hold values 0 or 1
Outputs:
- draft_out: bfloat16 [3008, 4096], P(('groups', 'tensor', 'dp')), parts along dimension 0
The draws below stay inside these ranges and needn't reach their ends.
There are 2 independent parts, one for each index of `groups`. The reference program is written for one: setup_inputs(seed, part) draws one part's arguments, and reference() takes and returns one part's arrays. A program takes and returns all parts, laid end to end along the dimension named above; an argument that names none is the same for every part. Nothing has to cross between parts.
Inputs may be any that keep to these rules, and one draw needn't show every extreme that they name: `owner_map`: in each data row every owner holds exactly two sequences, the sequences tile the row's 384 tokens in packing order, and the tokens of one row mapped to one owner number at most 94, reached by some owner in every row. offsets are the running sums of lengths in packing order.
All inputs are finite; a program needn't handle non-finite values. No bound on the sum of `loss_mask` on one device may be relied on, other than what follows from the above.
Results may differ from the reference program's by a relative error of at most 0.03.
Values may be sent and summed in bfloat16 or wider, within the bound.
A program may use at most 256 MiB of HBM per device.

```python
import math
import jax
import jax.numpy as jnp
from jax import lax

D = 8192
HF = 28672
QH = 32
KH = 4
HS = 128
TOK_DEV = 384
DROWS = 2
TOKENS = 768
CAP = 94
COLS = 5120
SLOTS = 1504
N_TENSOR = 8


def route_tables(key):
    owners = N_TENSOR
    mean_load = TOK_DEV // N_TENSOR

    def one_row(row_key):
        first_key, swing_key, pick_key, split_key, pack_key = jax.random.split(row_key, 5)
        order = jax.random.permutation(first_key, owners)
        swing = jax.random.randint(swing_key, (owners // 2,), -(mean_load - 2), mean_load - 1)
        chosen = jax.random.randint(pick_key, (), 0, owners // 2)
        swing = jnp.where(jnp.arange(owners // 2) == chosen, mean_load - 2, swing)
        pair_load = jnp.stack([mean_load + swing, mean_load - swing], axis=1).reshape(owners)
        load = jnp.zeros((owners,), jnp.int32).at[order].set(pair_load.astype(jnp.int32))
        first = jax.random.randint(split_key, (owners,), 0, 1 << 20) % (load - 1) + 1
        pieces = jnp.stack([first, load - first], axis=1).reshape(2 * owners)
        packing = jax.random.permutation(pack_key, 2 * owners)
        seq_lengths = pieces[packing].astype(jnp.int32)
        owner = (packing // 2).astype(jnp.int32)
        starts = (jnp.cumsum(seq_lengths) - seq_lengths).astype(jnp.int32)
        return (seq_lengths, starts, owner)
    keys = jax.random.split(key, DROWS)
    return jax.vmap(one_row)(keys)


def draw_lengths(key, part):
    return route_tables(key)[0]


def draw_offsets(key, part):
    return route_tables(key)[1]


def draw_owner_map(key, part):
    return route_tables(key)[2]


def set_ends(values, rng, least, top_value):
    longest = values.shape.index(max(values.shape))
    spots = []
    for shift in (0, 1):
        where = [jax.random.randint(jax.random.fold_in(rng, axis), (), 0, length) for axis, length in enumerate(values.shape)]
        where[longest] = (where[longest] + shift) % values.shape[longest]
        spots.append(tuple(where))
    return values.at[spots[0]].set(least).at[spots[1]].set(top_value)


def with_spikes(array, key, source, target, blocks, factor):
    owner, partner = [(jnp.arange(array.shape[dim]) // (array.shape[dim] // blocks)).reshape([-1 if axis == dim else 1 for axis in range(array.ndim)]) for dim in (source, target)]
    chosen = jax.random.permutation(key, blocks)[partner]
    strong = (owner == chosen) | (owner == (partner + blocks // 2) % blocks)
    return jnp.where(strong, factor * array, array)


def block_levels(key, dims, cuts, low, top_value):
    def one(axis_at, shards_of):
        draws = jax.random.uniform(jax.random.fold_in(jax.random.fold_in(key, 6), axis_at), (shards_of,), jnp.float32, low / len(cuts), top_value / len(cuts))
        return jnp.repeat(jnp.exp(draws), dims[axis_at] // shards_of).reshape((-1,) + (1,) * (len(dims) - axis_at - 1))

    factor_of = one(*cuts[0])
    for cut in cuts[1:]:
        factor_of = factor_of * one(*cut)
    return factor_of


def gaussian(rng, dims, deviation, limit, cuts=(), kind=jnp.bfloat16):
    level = block_levels(rng, dims, cuts, -0.22, 0.18) if cuts else 1.0
    drawn = jax.random.normal(rng, dims, jnp.float32) * deviation * level
    return jnp.minimum(jnp.maximum(drawn, -limit), limit).astype(kind)


def gaussian_with(rng, extent, deviation, reach, cuts, heavy, kind=jnp.bfloat16):
    drawn = deviation * jax.random.normal(rng, extent, jnp.float32)
    if cuts:
        drawn = drawn * block_levels(rng, extent, cuts, -0.22, 0.18)
    return jnp.clip(with_spikes(drawn, jax.random.fold_in(rng, 3), *heavy), -reach, reach).astype(kind)


def setup_inputs(seed: int = 0, part: int = 0) -> dict:
    key_of = jax.random.split(jax.random.key(seed), 13)
    part_splits = jax.random.split(jax.random.fold_in(key_of[12], part), 13)
    hidden_act = gaussian(part_splits[0], (TOKENS, HF), 1.0, 6.0, ((0, 2), (1, 8)))
    down_weight = gaussian_with(key_of[1], (HF, D), HF ** -0.5, 0.046875, ((0, 8), (1, 2)), (0, 1, 8, 2.0))
    residual = gaussian(part_splits[2], (TOKENS, D), 1.0, 6.0, ((0, 2), (1, 8)))
    tap_early = gaussian(part_splits[3], (TOKENS, D), 1.0, 6.0, ((0, 2), (1, 8)))
    tap_middle = gaussian(part_splits[4], (TOKENS, D), 1.0, 6.0, ((0, 2), (1, 8)))
    merge_weight = gaussian_with(key_of[5], (3, D, COLS), (3 * D) ** -0.5, 0.0546875, ((1, 8), (2, 2)), (1, 2, 8, 2.0))
    q_gain = jnp.clip(jax.random.uniform(key_of[6], (HS,), jnp.float32, 0.5, 2.0), 0.5, 2.0)
    k_gain = jnp.clip(jax.random.uniform(key_of[7], (HS,), jnp.float32, 0.5, 2.0), 0.5, 2.0)
    lengths = draw_lengths(jax.random.fold_in(jax.random.fold_in(key_of[12], part), 71), part)
    offsets = draw_offsets(jax.random.fold_in(jax.random.fold_in(key_of[12], part), 71), part)
    owner_map = draw_owner_map(jax.random.fold_in(jax.random.fold_in(key_of[12], part), 71), part)
    loss_mask = set_ends((jax.random.randint(part_splits[11], (TOKENS,), 0, 4) < 3).astype(jnp.int32), jax.random.fold_in(part_splits[11], 1), 0, 1)
    return dict(hidden_act=hidden_act, down_weight=down_weight, residual=residual, tap_early=tap_early, tap_middle=tap_middle, merge_weight=merge_weight, q_gain=q_gain, k_gain=k_gain, lengths=lengths, offsets=offsets, owner_map=owner_map, loss_mask=loss_mask)


def slot_map(lengths, offsets, owners, slot_owner, slot_pos):
    index = jnp.arange(lengths.shape[0], dtype=jnp.int32)
    earlier = (owners[None, :] == owners[:, None]) & (index[None, :] < index[:, None])
    base = lax.optimization_barrier(jnp.sum(jnp.where(earlier, lengths[None, :], 0), axis=1))
    hit = (owners[None, :] == slot_owner[:, None]) & (base[None, :] <= slot_pos[:, None]) & (slot_pos[:, None] < (base + lengths)[None, :])
    live = jnp.any(hit, axis=1)
    token = lax.optimization_barrier(jnp.sum(jnp.where(hit, (offsets - base)[None, :] + slot_pos[:, None], 0), axis=1))
    sequence = jnp.where(live, lax.optimization_barrier(jnp.sum(jnp.where(hit, index[None, :], 0), axis=1)), -1)
    return (token.astype(jnp.int32), live, sequence)

def attend(merged, live, sequence, keep, q_gain, k_gain):
    slots = merged.shape[0]
    query = merged[:, :QH * HS].astype(jnp.float32).reshape(slots, KH, QH // KH, HS)
    keys = merged[:, QH * HS:(QH + KH) * HS].astype(jnp.float32).reshape(slots, KH, HS)
    values = merged[:, (QH + KH) * HS:].astype(jnp.float32).reshape(slots, KH, HS)
    query = query * lax.rsqrt(lax.optimization_barrier(jnp.mean(query * query, axis=-1, keepdims=True)) + 1e-06) * q_gain
    keys = keys * lax.rsqrt(lax.optimization_barrier(jnp.mean(keys * keys, axis=-1, keepdims=True)) + 1e-06) * k_gain
    scores = jnp.einsum('qkgd,skd->kgqs', query, keys) / math.sqrt(HS)
    place = jnp.arange(slots, dtype=jnp.int32)
    allowed = (sequence[:, None] == sequence[None, :]) & live[None, :] & (place[None, :] <= place[:, None])
    scores = jnp.where(allowed, scores, -1e+30)
    top = lax.optimization_barrier(jnp.max(scores, axis=-1, keepdims=True))
    expo = jnp.exp(scores - top)
    weights = (expo / lax.optimization_barrier(jnp.sum(expo, axis=-1, keepdims=True))).astype(jnp.bfloat16)
    result = jnp.einsum('kgqs,skd->qkgd', weights.astype(jnp.float32), values)
    result = result.reshape(slots, QH * HS) * keep[:, None].astype(jnp.float32)
    return result.astype(jnp.bfloat16)

def down_block(total, operands):
    portion = jnp.dot(operands[0], operands[1], preferred_element_type=jnp.float32).astype(jnp.bfloat16)
    portion = lax.optimization_barrier(portion)
    return (total + portion.astype(jnp.float32), None)

def join_block(total, operands):
    portion = jnp.einsum('ntd,tdc->nc', operands[0].astype(jnp.float32), operands[1].astype(jnp.float32)).astype(jnp.bfloat16)
    portion = lax.optimization_barrier(portion)
    return (total + portion.astype(jnp.float32), None)

def reference(hidden_act, down_weight, residual, tap_early, tap_middle, merge_weight, q_gain, k_gain, lengths, offsets, owner_map, loss_mask):
    unit_width = HF // N_TENSOR
    left_blocks = hidden_act.reshape(TOKENS, N_TENSOR, unit_width).transpose(1, 0, 2)
    right_blocks = down_weight.reshape(N_TENSOR, unit_width, D)
    summed, unused = lax.scan(down_block, jnp.zeros((TOKENS, D), jnp.float32), (left_blocks, right_blocks))
    tap_late = (residual.astype(jnp.float32) + summed).astype(jnp.bfloat16)
    feature_width = D // N_TENSOR
    tap_blocks = jnp.stack([tap_early, tap_middle, tap_late], axis=1).reshape(TOKENS, 3, N_TENSOR, feature_width).transpose(2, 0, 1, 3)
    weight_blocks = merge_weight.reshape(3, N_TENSOR, feature_width, COLS).transpose(1, 0, 2, 3)
    joined, unused = lax.scan(join_block, jnp.zeros((TOKENS, COLS), jnp.float32), (tap_blocks, weight_blocks))
    merged = joined.astype(jnp.bfloat16)
    slot_owner = (jnp.arange(N_TENSOR * CAP, dtype=jnp.int32) // CAP).astype(jnp.int32)
    slot_pos = (jnp.arange(N_TENSOR * CAP, dtype=jnp.int32) % CAP).astype(jnp.int32)
    blocks = []
    for row in range(DROWS):
        token, live, sequence = slot_map(lengths[row], offsets[row], owner_map[row], slot_owner, slot_pos)
        where_token = (row * TOK_DEV + token).astype(jnp.int32)
        rows = merged[where_token]
        keep = live & (loss_mask[where_token] == 1)
        result = jax.vmap(attend, in_axes=(0, 0, 0, 0, None, None))(rows.reshape(N_TENSOR, CAP, COLS), live.reshape(N_TENSOR, CAP), sequence.reshape(N_TENSOR, CAP), keep.reshape(N_TENSOR, CAP), q_gain, k_gain)
        blocks.append(result)
    return jnp.stack(blocks, axis=1).reshape(SLOTS, QH * HS)
```

```python
import math

import jax
import jax.numpy as jnp
from jax import lax
from jax.sharding import PartitionSpec as P

QH = 32
KH = 4
HS = 128
BF = jnp.bfloat16
F32 = jnp.float32


def swap(x):
    return lax.ppermute(x, "dp", [(0, 1), (1, 0)])


def head_order(per_core, core):
    order = []
    group = QH // KH
    for k in range(KH):
        for g in range(group // (2 * per_core)):
            first = k * group + g * 2 * per_core + core * per_core
            order += list(range(first, first + per_core))
            order.append(QH + core * KH + k)
    return order


def columns(x, blocks):
    return jnp.concatenate([x[..., b * HS : (b + 1) * HS] for b in blocks], axis=-1)


def own_columns(weight, core, per_core):
    half = weight.shape[-1] // HS
    need = [sorted(set(head_order(per_core, c))) for c in (0, 1)]
    send = [[b - c * half for b in need[1 - c] if b // half == c] for c in (0, 1)]
    sent = jnp.where(core == 0, columns(weight, send[0]), columns(weight, send[1]))
    came = swap(sent)
    both = jnp.concatenate([weight, came], axis=-1)

    def arranged(c):
        place = {b: b - c * half for b in need[c] if b // half == c}
        place.update({b + (1 - c) * half: half + i for i, b in enumerate(send[1 - c])})
        return columns(both, [place[b] for b in head_order(per_core, c)])

    return jnp.where(core == 0, arranged(0), arranged(1))


def norm(x, gain):
    return x * lax.rsqrt(jnp.mean(x * x, axis=-1, keepdims=True) + 1e-06) * gain


def attend(query, key, value, sequence, keep, q_gain, k_gain):
    tokens, wide = query.shape
    query = norm(query.astype(F32).reshape(tokens, wide // HS, HS), q_gain)
    key = norm(key.astype(F32), k_gain)
    scores = jnp.einsum("qhd,sd->hqs", query, key) / math.sqrt(HS)
    place = jnp.arange(tokens, dtype=jnp.int32)
    allowed = (sequence[:, None] == sequence[None, :]) & (place[None, :] <= place[:, None])
    scores = jnp.where(allowed, scores, -1e30)
    expo = jnp.exp(scores - jnp.max(scores, axis=-1, keepdims=True))
    weights = (expo / jnp.sum(expo, axis=-1, keepdims=True)).astype(BF)
    result = jnp.einsum("hqs,sd->qhd", weights, value, preferred_element_type=F32)
    return (result.reshape(tokens, wide) * keep[:, None]).astype(BF)


def local(
    hidden_act,
    down_weight,
    residual,
    tap_early,
    tap_middle,
    merge_weight,
    q_gain,
    k_gain,
    lengths,
    offsets,
    owner_map,
    loss_mask,
):
    rows = hidden_act.shape[0]
    chips = lax.axis_size("tensor")
    capacity = 2 * rows // chips - 2
    core = lax.axis_index("dp")
    chip = lax.axis_index("tensor")
    per_core = QH // chips
    wide = (per_core + 1) * HS
    n_seq = lengths.shape[1]

    hidden = lax.all_gather(hidden_act, "dp", axis=0, tiled=True)
    table = jnp.concatenate([lengths[0], offsets[0], owner_map[0], loss_mask])
    tables = lax.all_gather(table, "dp", axis=0, tiled=False)
    taps = lax.all_gather(jnp.concatenate([tap_early, tap_middle], axis=1), "dp", axis=0, tiled=True)

    partial_sum = jnp.dot(hidden, down_weight, preferred_element_type=F32).astype(BF)
    partial_sum = lax.all_to_all(partial_sum, "dp", split_axis=0, concat_axis=1, tiled=True)
    summed = lax.psum_scatter(partial_sum, "tensor", scatter_dimension=1, tiled=True).astype(F32)
    tap_late = (residual.astype(F32) + summed).astype(BF)
    late = lax.all_gather(tap_late, "dp", axis=0, tiled=True)

    weight = own_columns(merge_weight, core, per_core)
    joined = jnp.dot(taps, weight[:2].reshape(-1, weight.shape[2]), preferred_element_type=F32)
    joined = (joined + jnp.dot(late, weight[2], preferred_element_type=F32)).astype(BF)
    joined = joined.reshape(2, rows, chips // 2, wide).transpose(2, 0, 1, 3)
    merged = lax.psum_scatter(
        joined.reshape(chips, rows, wide), "tensor", scatter_dimension=0, tiled=False
    )

    row = chip % 2
    mine = jnp.where(row == 0, tables[0], tables[1])
    length, offset, owner = [mine[i * n_seq : (i + 1) * n_seq] for i in range(3)]
    keep = (mine[3 * n_seq :] == 1).astype(F32)
    token = jnp.arange(rows, dtype=jnp.int32)
    inside = (offset[None, :] <= token[:, None]) & (token[:, None] < (offset + length)[None, :])
    sequence = jnp.sum(jnp.where(inside, jnp.arange(n_seq, dtype=jnp.int32)[None, :], 0), axis=1)
    index = jnp.arange(n_seq, dtype=jnp.int32)
    earlier = (owner[None, :] == owner[:, None]) & (index[None, :] < index[:, None])
    base = jnp.sum(jnp.where(earlier, length[None, :], 0), axis=1)
    start = owner * capacity + base - offset
    slot = token + jnp.sum(jnp.where(inside, start[None, :], 0), axis=1)
    place = (jnp.arange(chips * capacity, dtype=jnp.int32)[:, None] == slot[None, :]).astype(BF)

    query, mine_kv = merged[:, : per_core * HS], merged[:, per_core * HS :]
    other_kv = swap(mine_kv)
    key = jnp.where(core == 0, mine_kv, other_kv)
    value = jnp.where(core == 0, other_kv, mine_kv)
    result = attend(query, key, value, sequence, keep, q_gain, k_gain)
    slots = jnp.dot(place, result, preferred_element_type=F32).astype(BF)
    slots = lax.all_to_all(
        slots.reshape(chips, capacity, per_core * HS), "tensor", split_axis=0, concat_axis=0, tiled=True
    )
    slots = slots.reshape(chips // 2, 2, capacity, per_core * HS)
    first, second = slots[:, 0], slots[:, 1]
    own = jnp.where(core == 0, first, second)
    came = swap(jnp.where(core == 0, second, first))
    low = jnp.where(core == 0, own, came)
    high = jnp.where(core == 0, came, own)
    out = jnp.stack([low, high], axis=1)
    return out.transpose(2, 0, 1, 3).reshape(capacity, QH * HS)


def solution(mesh):
    return jax.shard_map(
        local,
        mesh=mesh,
        in_specs=(
            P(("groups", "dp"), "tensor"),
            P("tensor", "dp"),
            P(("groups", "dp"), "tensor"),
            P(("groups", "dp"), "tensor"),
            P(("groups", "dp"), "tensor"),
            P(None, "tensor", "dp"),
            P(),
            P(),
            P(("groups", "dp"), None),
            P(("groups", "dp"), None),
            P(("groups", "dp"), None),
            P(("groups", "dp")),
        ),
        out_specs=P(("groups", "tensor", "dp"), None),
        check_vma=False,
    )
```

```python
import math

import jax
import jax.numpy as jnp
from jax import lax
from jax.experimental import pallas as pl
from jax.experimental.pallas import tpu as pltpu
from jax.sharding import PartitionSpec as P

QH = 32
KH = 4
HS = 128
BF = jnp.bfloat16
F32 = jnp.float32
MESH = pl.DeviceIdType.MESH


def swap(x):
    return lax.ppermute(x, "dp", [(0, 1), (1, 0)])


def head_order(per_core, core):
    order = []
    group = QH // KH
    for k in range(KH):
        for g in range(group // (2 * per_core)):
            first = k * group + g * 2 * per_core + core * per_core
            order += list(range(first, first + per_core))
            order.append(QH + core * KH + k)
    return order


def columns(x, blocks):
    return jnp.concatenate([x[..., b * HS : (b + 1) * HS] for b in blocks], axis=-1)


def own_columns(weight, core, per_core):
    half = weight.shape[-1] // HS
    need = [sorted(set(head_order(per_core, c))) for c in (0, 1)]
    send = [[b - c * half for b in need[1 - c] if b // half == c] for c in (0, 1)]
    sent = jnp.where(core == 0, columns(weight, send[0]), columns(weight, send[1]))
    came = swap(sent)
    both = jnp.concatenate([weight, came], axis=-1)

    def arranged(c):
        place = {b: b - c * half for b in need[c] if b // half == c}
        place.update({b + (1 - c) * half: half + i for i, b in enumerate(send[1 - c])})
        return columns(both, [place[b] for b in head_order(per_core, c)])

    return jnp.where(core == 0, arranged(0), arranged(1))


def norm(x, gain):
    return x * lax.rsqrt(jnp.mean(x * x, axis=-1, keepdims=True) + 1e-06) * gain


def attend(query, key, value, sequence, keep, q_gain, k_gain):
    tokens, wide = query.shape
    query = norm(query.astype(F32).reshape(tokens, wide // HS, HS), q_gain)
    key = norm(key.astype(F32), k_gain)
    scores = jnp.einsum("qhd,sd->hqs", query, key) / math.sqrt(HS)
    place = jnp.arange(tokens, dtype=jnp.int32)
    allowed = (sequence[:, None] == sequence[None, :]) & (place[None, :] <= place[:, None])
    scores = jnp.where(allowed, scores, -1e30)
    expo = jnp.exp(scores - jnp.max(scores, axis=-1, keepdims=True))
    weights = (expo / jnp.sum(expo, axis=-1, keepdims=True)).astype(BF)
    result = jnp.einsum("hqs,sd->qhd", weights, value, preferred_element_type=F32)
    return (result.reshape(tokens, wide) * keep[:, None]).astype(BF)


TILE = 256


def matmul(a, b):
    return jnp.dot(a, b, preferred_element_type=F32)


def greet(z, y, core):
    barrier = pltpu.get_barrier_semaphore()
    pl.semaphore_signal(barrier, 1, device_id={"tensor": z * 2 + 1 - y}, device_id_type=MESH)
    pl.semaphore_signal(barrier, 1, device_id={"dp": 1 - core}, device_id_type=MESH)

    @pl.when(z > 0)
    def _():
        pl.semaphore_signal(barrier, 1, device_id={"tensor": (z - 1) * 2 + y}, device_id_type=MESH)

    @pl.when(z < 3)
    def _():
        pl.semaphore_signal(barrier, 1, device_id={"tensor": (z + 1) * 2 + y}, device_id_type=MESH)

    pl.semaphore_wait(barrier, jnp.where((z == 0) | (z == 3), 3, 4))


def reduce_units(count, z, y, dest, product, finish, yout, own, yin, zin, sems):
    y_send, y_recv, z_send, z_recv = sems

    def y_copy(u):
        return pltpu.make_async_remote_copy(
            yout.at[u], yin.at[u], y_send.at[u], y_recv.at[u],
            device_id={"tensor": z * 2 + 1 - y}, device_id_type=MESH,
        )

    def z_copy(u, way):
        target = (z + 1 + 2 * way) % 4
        return pltpu.make_async_remote_copy(
            own.at[u], zin.at[way, u], z_send.at[u], z_recv.at[way, u],
            device_id={"tensor": target * 2 + y}, device_id_type=MESH,
        )

    def first(u, _):
        yout[u] = product(u, 0).astype(BF)
        y_copy(u).start()
        return 0

    lax.fori_loop(0, count, first, 0)

    def pass_on(i, way, place, edge):
        u = i - place

        @pl.when((u >= 0) & (u < count))
        def _():
            ahead = dest(u) - z if way == 0 else z - dest(u)

            @pl.when(ahead > 0)
            def _():
                y_copy(u).wait_recv()

                @pl.when(z == edge)
                def _():
                    own[u] = (own[u].astype(F32) + yin[u].astype(F32)).astype(BF)

                @pl.when(z != edge)
                def _():
                    z_copy(u, way).wait_recv()
                    total = own[u].astype(F32) + yin[u].astype(F32) + zin[way, u].astype(F32)
                    own[u] = total.astype(BF)

                z_copy(u, way).start()

    def second(i, _):
        @pl.when(i < count)
        def _():
            own[i] = product(i, 1).astype(BF)

        pass_on(i, 0, z, 0)
        pass_on(i, 1, 3 - z, 3)
        u = i - 3

        @pl.when(u >= 0)
        def _():
            @pl.when(dest(u) == z)
            def _():
                y_copy(u).wait_recv()

                @pl.when(z == 0)
                def _():
                    z_copy(u, 1).wait_recv()
                    finish(u, own[u].astype(F32) + yin[u].astype(F32) + zin[1, u].astype(F32))

                @pl.when(z == 3)
                def _():
                    z_copy(u, 0).wait_recv()
                    finish(u, own[u].astype(F32) + yin[u].astype(F32) + zin[0, u].astype(F32))

                @pl.when((z > 0) & (z < 3))
                def _():
                    z_copy(u, 0).wait_recv()
                    z_copy(u, 1).wait_recv()
                    total = own[u].astype(F32) + yin[u].astype(F32)
                    finish(u, total + zin[0, u].astype(F32) + zin[1, u].astype(F32))

        return 0

    lax.fori_loop(0, count + 3, second, 0)

    def last(u, _):
        y_copy(u).wait_send()

        @pl.when(dest(u) != z)
        def _():
            z_copy(u, 0).wait_send()

        return 0

    lax.fori_loop(0, count, last, 0)


def down_kernel(
    hidden_ref, weight_ref, residual_ref, early_ref, middle_ref, taps_ref,
    hidden, weight, res, yout, own, yin, zin,
    w_sem, in_sem, far_send, far_recv, y_send, y_recv, z_send, z_recv, out_send, out_recv,
):
    rows, width = residual_ref.shape
    tiles = width // TILE
    count = 4 * tiles
    chip, core = lax.axis_index("tensor"), lax.axis_index("dp")
    z, y = chip // 2, chip % 2
    other = {"dp": 1 - core}
    mine = pl.ds(pl.multiple_of(core * rows, rows), rows)

    def fetch(s):
        u, stage = s % count, s // count
        block = 2 * (u % 2) + (1 - y) * (1 - stage) + y * stage
        column = block * width + (u // 2) % tiles * TILE
        source = weight_ref.at[:, pl.ds(pl.multiple_of(column, TILE), TILE)]
        return pltpu.make_async_copy(source, weight.at[s % 2], w_sem.at[s % 2])

    near = [
        pltpu.make_async_copy(hidden_ref, hidden.at[0], in_sem.at[0]),
        pltpu.make_async_copy(residual_ref, res.at[0], in_sem.at[1]),
        pltpu.make_async_copy(early_ref, taps_ref.at[0, mine], in_sem.at[2]),
        pltpu.make_async_copy(middle_ref, taps_ref.at[1, mine], in_sem.at[3]),
    ]
    near[0].start()
    fetch(0).start()
    greet(z, y, core)
    pairs = [
        (hidden_ref, hidden.at[1]),
        (residual_ref, res.at[1]),
        (early_ref, taps_ref.at[0, mine]),
        (middle_ref, taps_ref.at[1, mine]),
    ]
    far = [
        pltpu.make_async_remote_copy(
            a, b, far_send.at[i], far_recv.at[i], device_id=other, device_id_type=MESH
        )
        for i, (a, b) in enumerate(pairs)
    ]
    far[0].start()
    for copy in near[1:]:
        copy.start()
    near[0].wait()
    for copy in far[1:]:
        copy.start()

    def product(u, stage):
        s = stage * count + u

        @pl.when(s == count // 2)
        def _():
            far[0].wait_recv()

        fetch(s).wait()

        @pl.when(s + 1 < 2 * count)
        def _():
            fetch(s + 1).start()

        return matmul(hidden[u // (count // 2)], weight[s % 2])

    def out_copy(u, source_core):
        half = (source_core + u // (count // 2)) % 2
        place = taps_ref.at[
            2,
            pl.ds(pl.multiple_of(half * rows, rows), rows),
            pl.ds(pl.multiple_of((u // 2) % tiles * TILE, TILE), TILE),
        ]
        return pltpu.make_async_remote_copy(
            place, place, out_send.at[u // 2], out_recv.at[u // 2], device_id=other, device_id_type=MESH
        )

    near[1].wait()
    far[1].wait_recv()

    def finish(u, total):
        half = (core + u // (count // 2)) % 2
        column = pl.ds(pl.multiple_of((u // 2) % tiles * TILE, TILE), TILE)
        late = total + res[u // (count // 2), :, column].astype(F32)
        taps_ref[2, pl.ds(pl.multiple_of(half * rows, rows), rows), column] = late.astype(BF)
        out_copy(u, core).start()

    sems = (y_send, y_recv, z_send, z_recv)
    reduce_units(
        count, z, y, lambda u: 2 * core + u % 2, product, finish, yout, own, yin, zin, sems
    )

    def close(r, _):
        @pl.when(z // 2 == core)
        def _():
            out_copy(2 * r, core).wait_send()

        @pl.when(z // 2 != core)
        def _():
            out_copy(2 * r, 1 - core).wait_recv()

        return 0

    lax.fori_loop(0, count // 2, close, 0)
    for copy in near[2:]:
        copy.wait()
    for copy in far:
        copy.wait_send()
    for copy in far[2:]:
        copy.wait_recv()


def join_kernel(
    taps_ref, weight_ref, merged_ref,
    weight, yout, own, yin, zin,
    w_sem, y_send, y_recv, z_send, z_recv, out_send, out_recv,
):
    rows = merged_ref.shape[1]
    count = weight_ref.shape[2] // TILE
    chip, core = lax.axis_index("tensor"), lax.axis_index("dp")
    z, y = chip // 2, chip % 2
    other = {"dp": 1 - core}

    def dest(u, c):
        high = jnp.where(u < 2, 2, jnp.where(u < 6, 3, u - 6))
        return jnp.where(c == 0, u // 4, high)

    def spot(u, c):
        high = jnp.where(u < 2, u + 2, jnp.where(u < 6, u - 2, 4))
        return jnp.where(c == 0, u % 4, high)

    def fetch(s):
        u = s % count
        pair = (core == 1) & (u >= 6)
        parts = (jnp.where(pair, u + 6, 2 * u), jnp.where(pair, u + 10, 2 * u + 1))
        return [
            pltpu.make_async_copy(
                weight_ref.at[:, :, pl.ds(pl.multiple_of(part * HS, HS), HS)],
                weight.at[s % 2, :, :, pl.ds(i * HS, HS)],
                w_sem.at[s % 2, i],
            )
            for i, part in enumerate(parts)
        ]

    for copy in fetch(0):
        copy.start()
    greet(z, y, core)

    def product(u, stage):
        s = stage * count + u
        for copy in fetch(s):
            copy.wait()

        @pl.when(s + 1 < 2 * count)
        def _():
            for copy in fetch(s + 1):
                copy.start()

        row = y if stage else 1 - y
        part = pl.ds(pl.multiple_of(row * rows, rows), rows)
        total = matmul(taps_ref[0, part], weight[s % 2, 0])
        total += matmul(taps_ref[1, part], weight[s % 2, 1])
        return total + matmul(taps_ref[2, part], weight[s % 2, 2])

    def out_copy(u, c):
        place = merged_ref.at[spot(u, c)]
        return pltpu.make_async_remote_copy(
            place, place, out_send.at[u], out_recv.at[u], device_id=other, device_id_type=MESH
        )

    def finish(u, total):
        merged_ref[spot(u, core)] = total.astype(BF)
        out_copy(u, core).start()

    sems = (y_send, y_recv, z_send, z_recv)
    reduce_units(
        count, z, y, lambda u: dest(u, core), product, finish, yout, own, yin, zin, sems
    )

    def close(u, _):
        @pl.when(dest(u, core) == z)
        def _():
            out_copy(u, core).wait_send()

        @pl.when(dest(u, 1 - core) == z)
        def _():
            out_copy(u, 1 - core).wait_recv()

        return 0

    lax.fori_loop(0, count, close, 0)


def units(count, rows):
    shape = (rows, TILE)
    return [
        pltpu.VMEM((count, *shape), BF),
        pltpu.VMEM((count, *shape), BF),
        pltpu.VMEM((count, *shape), BF),
        pltpu.VMEM((2, count, *shape), BF),
    ]


def dma(*shape):
    return pltpu.SemaphoreType.DMA(shape)


def unit_sems(count):
    return [dma(count), dma(count), dma(count), dma(2, count)]


def down_and_sum(hidden_act, down_weight, residual, tap_early, tap_middle):
    rows, units_in = hidden_act.shape
    width = residual.shape[1]
    count = 4 * width // TILE
    return pl.pallas_call(
        down_kernel,
        out_shape=jax.ShapeDtypeStruct((3, 2 * rows, width), BF),
        in_specs=[pl.BlockSpec(memory_space=pl.ANY)] * 5,
        out_specs=pl.BlockSpec(memory_space=pltpu.VMEM),
        scratch_shapes=[
            pltpu.VMEM((2, rows, units_in), BF),
            pltpu.VMEM((2, units_in, TILE), BF),
            pltpu.VMEM((2, rows, width), BF),
            *units(count, rows),
            dma(2), dma(4), dma(4), dma(4),
            *unit_sems(count),
            dma(count // 2), dma(count // 2),
        ],
        compiler_params=pltpu.CompilerParams(
            collective_id=0, has_side_effects=True, vmem_limit_bytes=56 << 20
        ),
        cost_estimate=pl.CostEstimate(
            flops=4 * rows * units_in * down_weight.shape[1],
            bytes_accessed=4 * down_weight.size,
            transcendentals=0,
        ),
        name="down_and_sum",
    )(hidden_act, down_weight, residual, tap_early, tap_middle)


def join_and_sum(taps, merge_weight):
    rows = taps.shape[1] // 2
    parts, depth, wide = merge_weight.shape
    count = wide // TILE
    return pl.pallas_call(
        join_kernel,
        out_shape=jax.ShapeDtypeStruct((5, rows, TILE), BF),
        in_specs=[pl.BlockSpec(memory_space=pltpu.VMEM), pl.BlockSpec(memory_space=pl.ANY)],
        out_specs=pl.BlockSpec(memory_space=pltpu.VMEM),
        scratch_shapes=[
            pltpu.VMEM((2, parts, depth, TILE), BF),
            *units(count, rows),
            dma(2, 2),
            *unit_sems(count),
            dma(count), dma(count),
        ],
        compiler_params=pltpu.CompilerParams(
            collective_id=1, has_side_effects=True, vmem_limit_bytes=56 << 20
        ),
        cost_estimate=pl.CostEstimate(
            flops=4 * rows * parts * depth * wide,
            bytes_accessed=4 * merge_weight.size,
            transcendentals=0,
        ),
        name="join_and_sum",
    )(taps, merge_weight)


def plain_sums(hidden_act, down_weight, residual, tap_early, tap_middle, merge_weight):
    rows = hidden_act.shape[0]
    chips = lax.axis_size("tensor")
    core = lax.axis_index("dp")
    per_core = QH // chips
    wide = (per_core + 1) * HS
    hidden = lax.all_gather(hidden_act, "dp", axis=0, tiled=True)
    taps = lax.all_gather(jnp.concatenate([tap_early, tap_middle], axis=1), "dp", axis=0, tiled=True)
    partial_sum = jnp.dot(hidden, down_weight, preferred_element_type=F32).astype(BF)
    partial_sum = lax.all_to_all(partial_sum, "dp", split_axis=0, concat_axis=1, tiled=True)
    summed = lax.psum_scatter(partial_sum, "tensor", scatter_dimension=1, tiled=True).astype(F32)
    tap_late = (residual.astype(F32) + summed).astype(BF)
    late = lax.all_gather(tap_late, "dp", axis=0, tiled=True)

    weight = own_columns(merge_weight, core, per_core)
    joined = jnp.dot(taps, weight[:2].reshape(-1, weight.shape[2]), preferred_element_type=F32)
    joined = (joined + jnp.dot(late, weight[2], preferred_element_type=F32)).astype(BF)
    joined = joined.reshape(2, rows, chips // 2, wide).transpose(2, 0, 1, 3)
    merged = lax.psum_scatter(
        joined.reshape(chips, rows, wide), "tensor", scatter_dimension=0, tiled=False
    )
    query, mine_kv = merged[:, : per_core * HS], merged[:, per_core * HS :]
    other_kv = swap(mine_kv)
    key = jnp.where(core == 0, mine_kv, other_kv)
    value = jnp.where(core == 0, other_kv, mine_kv)
    return query, key, value


def chain_sums(hidden_act, down_weight, residual, tap_early, tap_middle, merge_weight):
    taps = down_and_sum(hidden_act, down_weight, residual, tap_early, tap_middle)
    merged = join_and_sum(taps, merge_weight)
    query = jnp.where(lax.axis_index("dp") == 0, merged[:2], merged[2:4])
    query = jnp.concatenate([query[0], query[1]], axis=1)
    return query, merged[4, :, :HS], merged[4, :, HS:]


def local(
    hidden_act,
    down_weight,
    residual,
    tap_early,
    tap_middle,
    merge_weight,
    q_gain,
    k_gain,
    lengths,
    offsets,
    owner_map,
    loss_mask,
):
    rows = hidden_act.shape[0]
    chips = lax.axis_size("tensor")
    capacity = 2 * rows // chips - 2
    core = lax.axis_index("dp")
    chip = lax.axis_index("tensor")
    per_core = QH // chips
    n_seq = lengths.shape[1]

    table = jnp.concatenate([lengths[0], offsets[0], owner_map[0], loss_mask])
    tables = lax.all_gather(table, "dp", axis=0, tiled=False)
    sums = chain_sums if chips == 8 else plain_sums
    query, key, value = sums(hidden_act, down_weight, residual, tap_early, tap_middle, merge_weight)

    row = chip % 2
    mine = jnp.where(row == 0, tables[0], tables[1])
    length, offset, owner = [mine[i * n_seq : (i + 1) * n_seq] for i in range(3)]
    keep = (mine[3 * n_seq :] == 1).astype(F32)
    token = jnp.arange(rows, dtype=jnp.int32)
    inside = (offset[None, :] <= token[:, None]) & (token[:, None] < (offset + length)[None, :])
    sequence = jnp.sum(jnp.where(inside, jnp.arange(n_seq, dtype=jnp.int32)[None, :], 0), axis=1)
    index = jnp.arange(n_seq, dtype=jnp.int32)
    earlier = (owner[None, :] == owner[:, None]) & (index[None, :] < index[:, None])
    base = jnp.sum(jnp.where(earlier, length[None, :], 0), axis=1)
    start = owner * capacity + base - offset
    slot = token + jnp.sum(jnp.where(inside, start[None, :], 0), axis=1)
    place = (jnp.arange(chips * capacity, dtype=jnp.int32)[:, None] == slot[None, :]).astype(BF)

    result = attend(query, key, value, sequence, keep, q_gain, k_gain)
    slots = jnp.dot(place, result, preferred_element_type=F32).astype(BF)
    slots = lax.all_to_all(
        slots.reshape(chips, capacity, per_core * HS), "tensor", split_axis=0, concat_axis=0, tiled=True
    )
    slots = slots.reshape(chips // 2, 2, capacity, per_core * HS)
    first, second = slots[:, 0], slots[:, 1]
    own = jnp.where(core == 0, first, second)
    came = swap(jnp.where(core == 0, second, first))
    low = jnp.where(core == 0, own, came)
    high = jnp.where(core == 0, came, own)
    out = jnp.stack([low, high], axis=1)
    return out.transpose(2, 0, 1, 3).reshape(capacity, QH * HS)


def solution(mesh):
    return jax.shard_map(
        local,
        mesh=mesh,
        in_specs=(
            P(("groups", "dp"), "tensor"),
            P("tensor", "dp"),
            P(("groups", "dp"), "tensor"),
            P(("groups", "dp"), "tensor"),
            P(("groups", "dp"), "tensor"),
            P(None, "tensor", "dp"),
            P(),
            P(),
            P(("groups", "dp"), None),
            P(("groups", "dp"), None),
            P(("groups", "dp"), None),
            P(("groups", "dp")),
        ),
        out_specs=P(("groups", "tensor", "dp"), None),
        check_vma=False,
    )
```

```python
import math

import jax
import jax.numpy as jnp
from jax import lax
from jax.experimental import pallas as pl
from jax.experimental.pallas import tpu as pltpu
from jax.sharding import PartitionSpec as P

QH = 32
KH = 4
HS = 128
BF = jnp.bfloat16
F32 = jnp.float32
MESH = pl.DeviceIdType.MESH


def swap(x):
    return lax.ppermute(x, "dp", [(0, 1), (1, 0)])


def head_order(per_core, core):
    order = []
    group = QH // KH
    for k in range(KH):
        for g in range(group // (2 * per_core)):
            first = k * group + g * 2 * per_core + core * per_core
            order += list(range(first, first + per_core))
            order.append(QH + core * KH + k)
    return order


def columns(x, blocks):
    return jnp.concatenate([x[..., b * HS : (b + 1) * HS] for b in blocks], axis=-1)


def own_columns(weight, core, per_core):
    half = weight.shape[-1] // HS
    need = [sorted(set(head_order(per_core, c))) for c in (0, 1)]
    send = [[b - c * half for b in need[1 - c] if b // half == c] for c in (0, 1)]
    sent = jnp.where(core == 0, columns(weight, send[0]), columns(weight, send[1]))
    came = swap(sent)
    both = jnp.concatenate([weight, came], axis=-1)

    def arranged(c):
        place = {b: b - c * half for b in need[c] if b // half == c}
        place.update({b + (1 - c) * half: half + i for i, b in enumerate(send[1 - c])})
        return columns(both, [place[b] for b in head_order(per_core, c)])

    return jnp.where(core == 0, arranged(0), arranged(1))


def norm(x, gain):
    return x * lax.rsqrt(jnp.mean(x * x, axis=-1, keepdims=True) + 1e-06) * gain


def attend(query, key, value, sequence, keep, q_gain, k_gain):
    tokens, wide = query.shape
    query = norm(query.astype(F32).reshape(tokens, wide // HS, HS), q_gain)
    key = norm(key.astype(F32), k_gain)
    scores = jnp.einsum("qhd,sd->hqs", query, key) / math.sqrt(HS)
    place = jnp.arange(tokens, dtype=jnp.int32)
    allowed = (sequence[:, None] == sequence[None, :]) & (place[None, :] <= place[:, None])
    scores = jnp.where(allowed, scores, -1e30)
    expo = jnp.exp(scores - jnp.max(scores, axis=-1, keepdims=True))
    weights = (expo / jnp.sum(expo, axis=-1, keepdims=True)).astype(BF)
    result = jnp.einsum("hqs,sd->qhd", weights, value, preferred_element_type=F32)
    return (result.reshape(tokens, wide) * keep[:, None]).astype(BF)


TILE = 256


def matmul(a, b):
    return jnp.dot(a, b, preferred_element_type=F32)


def greet(me):
    barrier = pltpu.get_barrier_semaphore()

    def signal(i, _):
        peer = (me + i) % 16
        pl.semaphore_signal(
            barrier, 1, device_id={"tensor": peer // 2, "dp": peer % 2}, device_id_type=MESH
        )
        return 0

    lax.fori_loop(1, 16, signal, 0)
    pl.semaphore_wait(barrier, 15)


def reduce_units(count, z, y, dest, product, finish, yout, own, yin, zin, sems):
    y_send, y_recv, z_send, z_recv = sems

    def y_copy(u):
        return pltpu.make_async_remote_copy(
            yout.at[u], yin.at[u], y_send.at[u], y_recv.at[u],
            device_id={"tensor": z * 2 + 1 - y}, device_id_type=MESH,
        )

    def z_copy(u, way):
        target = (z + 1 + 2 * way) % 4
        return pltpu.make_async_remote_copy(
            own.at[u], zin.at[way, u], z_send.at[u], z_recv.at[way, u],
            device_id={"tensor": target * 2 + y}, device_id_type=MESH,
        )

    def first(u, _):
        yout[u] = product(u, 0).astype(BF)
        y_copy(u).start()
        return 0

    lax.fori_loop(0, count, first, 0)

    def pass_on(i, way, place, edge):
        u = i - place

        @pl.when((u >= 0) & (u < count))
        def _():
            ahead = dest(u) - z if way == 0 else z - dest(u)

            @pl.when(ahead > 0)
            def _():
                y_copy(u).wait_recv()

                @pl.when(z == edge)
                def _():
                    own[u] = (own[u].astype(F32) + yin[u].astype(F32)).astype(BF)

                @pl.when(z != edge)
                def _():
                    z_copy(u, way).wait_recv()
                    total = own[u].astype(F32) + yin[u].astype(F32) + zin[way, u].astype(F32)
                    own[u] = total.astype(BF)

                z_copy(u, way).start()

    def second(i, _):
        @pl.when(i < count)
        def _():
            own[i] = product(i, 1).astype(BF)

        pass_on(i, 0, z, 0)
        pass_on(i, 1, 3 - z, 3)
        u = i - 3

        @pl.when(u >= 0)
        def _():
            @pl.when(dest(u) == z)
            def _():
                y_copy(u).wait_recv()

                @pl.when(z == 0)
                def _():
                    z_copy(u, 1).wait_recv()
                    finish(u, own[u].astype(F32) + yin[u].astype(F32) + zin[1, u].astype(F32))

                @pl.when(z == 3)
                def _():
                    z_copy(u, 0).wait_recv()
                    finish(u, own[u].astype(F32) + yin[u].astype(F32) + zin[0, u].astype(F32))

                @pl.when((z > 0) & (z < 3))
                def _():
                    z_copy(u, 0).wait_recv()
                    z_copy(u, 1).wait_recv()
                    total = own[u].astype(F32) + yin[u].astype(F32)
                    finish(u, total + zin[0, u].astype(F32) + zin[1, u].astype(F32))

        return 0

    lax.fori_loop(0, count + 3, second, 0)

    def last(u, _):
        y_copy(u).wait_send()

        @pl.when(dest(u) != z)
        def _():
            z_copy(u, 0).wait_send()

        return 0

    lax.fori_loop(0, count, last, 0)


def down_part(
    ins, taps_ref, hidden, weight, res, tab, yout, own, yin, zin,
    w_sem, in_sem, far_send, far_recv, y_send, y_recv, z_send, z_recv, out_send, out_recv, warm_up,
):
    hidden_ref, weight_ref, residual_ref, early_ref, middle_ref = ins
    rows, width = residual_ref.shape
    tiles = width // TILE
    count = 4 * tiles
    chip, core = lax.axis_index("tensor"), lax.axis_index("dp")
    z, y = chip // 2, chip % 2
    other = {"dp": 1 - core}
    mine = pl.ds(pl.multiple_of(core * rows, rows), rows)

    def fetch(s):
        u, stage = s % count, s // count
        block = 2 * (u % 2) + (1 - y) * (1 - stage) + y * stage
        column = block * width + (u // 2) % tiles * TILE
        source = weight_ref.at[:, pl.ds(pl.multiple_of(column, TILE), TILE)]
        return pltpu.make_async_copy(source, weight.at[s % 2], w_sem.at[s % 2])

    near = [
        pltpu.make_async_copy(hidden_ref, hidden.at[0], in_sem.at[0]),
        pltpu.make_async_copy(residual_ref, res.at[0], in_sem.at[1]),
        pltpu.make_async_copy(early_ref, taps_ref.at[0, mine], in_sem.at[2]),
        pltpu.make_async_copy(middle_ref, taps_ref.at[1, mine], in_sem.at[3]),
    ]
    near[0].start()
    fetch(0).start()
    warm_up()
    greet(chip * 2 + core)
    pairs = [
        (hidden_ref, hidden.at[1]),
        (residual_ref, res.at[1]),
        (early_ref, taps_ref.at[0, mine]),
        (middle_ref, taps_ref.at[1, mine]),
        (tab.at[0], tab.at[1]),
    ]
    far = [
        pltpu.make_async_remote_copy(
            a, b, far_send.at[i], far_recv.at[i], device_id=other, device_id_type=MESH
        )
        for i, (a, b) in enumerate(pairs)
    ]
    far[0].start()
    for copy in near[1:]:
        copy.start()
    near[0].wait()
    for copy in far[1:]:
        copy.start()

    def product(u, stage):
        s = stage * count + u

        @pl.when(s == count // 2)
        def _():
            far[0].wait_recv()

        fetch(s).wait()

        @pl.when(s + 1 < 2 * count)
        def _():
            fetch(s + 1).start()

        return matmul(hidden[u // (count // 2)], weight[s % 2])

    def out_copy(u, source_core):
        half = (source_core + u // (count // 2)) % 2
        place = taps_ref.at[
            2,
            pl.ds(pl.multiple_of(half * rows, rows), rows),
            pl.ds(pl.multiple_of((u // 2) % tiles * TILE, TILE), TILE),
        ]
        return pltpu.make_async_remote_copy(
            place, place, out_send.at[u // 2], out_recv.at[u // 2], device_id=other, device_id_type=MESH
        )

    near[1].wait()
    far[1].wait_recv()

    def finish(u, total):
        half = (core + u // (count // 2)) % 2
        column = pl.ds(pl.multiple_of((u // 2) % tiles * TILE, TILE), TILE)
        late = total + res[u // (count // 2), :, column].astype(F32)
        taps_ref[2, pl.ds(pl.multiple_of(half * rows, rows), rows), column] = late.astype(BF)
        out_copy(u, core).start()

    sems = (y_send, y_recv, z_send, z_recv)
    reduce_units(
        count, z, y, lambda u: 2 * core + u % 2, product, finish, yout, own, yin, zin, sems
    )

    def close(r, _):
        @pl.when(z // 2 == core)
        def _():
            out_copy(2 * r, core).wait_send()

        @pl.when(z // 2 != core)
        def _():
            out_copy(2 * r, 1 - core).wait_recv()

        return 0

    lax.fori_loop(0, count // 2, close, 0)
    for copy in near[2:]:
        copy.wait()
    for copy in far:
        copy.wait_send()
    for copy in far[2:]:
        copy.wait_recv()


def join_fetch(s, count, core, weight_ref, weight, w_sem):
    u = s % count
    pair = (core == 1) & (u >= 6)
    parts = (jnp.where(pair, u + 6, 2 * u), jnp.where(pair, u + 10, 2 * u + 1))
    return [
        pltpu.make_async_copy(
            weight_ref.at[:, :, pl.ds(pl.multiple_of(part * HS, HS), HS)],
            weight.at[s % 2, :, :, pl.ds(i * HS, HS)],
            w_sem.at[s % 2, i],
        )
        for i, part in enumerate(parts)
    ]


def join_part(
    taps_ref, weight_ref, merged_ref, weight, yout, own, yin, zin,
    w_sem, y_send, y_recv, z_send, z_recv, out_send, out_recv,
):
    rows = merged_ref.shape[1]
    count = weight_ref.shape[2] // TILE
    chip, core = lax.axis_index("tensor"), lax.axis_index("dp")
    z, y = chip // 2, chip % 2
    other = {"dp": 1 - core}

    def dest(u, c):
        high = jnp.where(u < 2, 2, jnp.where(u < 6, 3, u - 6))
        return jnp.where(c == 0, u // 4, high)

    def spot(u, c):
        high = jnp.where(u < 2, u + 2, jnp.where(u < 6, u - 2, 4))
        return jnp.where(c == 0, u % 4, high)

    def fetch(s):
        return join_fetch(s, count, core, weight_ref, weight, w_sem)

    def product(u, stage):
        s = stage * count + u
        for copy in fetch(s):
            copy.wait()

        @pl.when(s + 1 < 2 * count)
        def _():
            for copy in fetch(s + 1):
                copy.start()

        row = y if stage else 1 - y
        part = pl.ds(pl.multiple_of(row * rows, rows), rows)
        total = matmul(taps_ref[0, part], weight[s % 2, 0])
        total += matmul(taps_ref[1, part], weight[s % 2, 1])
        return total + matmul(taps_ref[2, part], weight[s % 2, 2])

    def out_copy(u, c):
        place = merged_ref.at[spot(u, c)]
        return pltpu.make_async_remote_copy(
            place, place, out_send.at[u], out_recv.at[u], device_id=other, device_id_type=MESH
        )

    def finish(u, total):
        merged_ref[spot(u, core)] = total.astype(BF)
        out_copy(u, core).start()

    sems = (y_send, y_recv, z_send, z_recv)
    reduce_units(
        count, z, y, lambda u: dest(u, core), product, finish, yout, own, yin, zin, sems
    )

    def close(u, _):
        @pl.when(dest(u, core) == z)
        def _():
            out_copy(u, core).wait_send()

        @pl.when(dest(u, 1 - core) == z)
        def _():
            out_copy(u, 1 - core).wait_recv()

        return 0

    lax.fori_loop(0, count, close, 0)


def attend_part(
    merged_ref, tab, q_gain_ref, k_gain_ref, out_ref, result, slots, slot_send, slot_recv, n_seq, capacity
):
    rows = merged_ref.shape[1]
    chip, core = lax.axis_index("tensor"), lax.axis_index("dp")
    z, y = chip // 2, chip % 2
    table = tab[(core + y) % 2]
    length, offset, owner = [table[i : i + 1, :n_seq] for i in range(3)]
    keep = table[3:4]
    across = lax.broadcasted_iota(jnp.int32, (n_seq, n_seq), 1)
    down = lax.broadcasted_iota(jnp.int32, (n_seq, n_seq), 0)

    def upright(x):
        return jnp.sum(jnp.where(across == down, x, 0), axis=1, keepdims=True)

    length_up, offset_up, owner_up = upright(length), upright(offset), upright(owner)
    earlier = (owner == owner_up) & (across < down)
    base_up = jnp.sum(jnp.where(earlier, length, 0), axis=1, keepdims=True)
    start_up = owner_up * capacity + base_up - offset_up
    token = lax.broadcasted_iota(jnp.int32, (n_seq, rows), 1)
    inside = (offset_up <= token) & (token < offset_up + length_up)
    index = lax.broadcasted_iota(jnp.int32, (n_seq, rows), 0)
    sequence = jnp.sum(jnp.where(inside, index, 0), axis=0, keepdims=True)
    slot = jnp.sum(jnp.where(inside, start_up + token, 0), axis=0, keepdims=True)
    slot = jnp.where(keep == 1, slot, -1)
    token_up = lax.broadcasted_iota(jnp.int32, (rows, n_seq), 0)
    inside_up = (offset <= token_up) & (token_up < offset + length)
    index_up = lax.broadcasted_iota(jnp.int32, (rows, n_seq), 1)
    sequence_up = jnp.sum(jnp.where(inside_up, index_up, 0), axis=1, keepdims=True)
    later = lax.broadcasted_iota(jnp.int32, (rows, rows), 0)
    place = lax.broadcasted_iota(jnp.int32, (rows, rows), 1)
    allowed = (sequence_up == sequence) & (place <= later)

    key = norm(merged_ref[4, :, :HS].astype(F32), k_gain_ref[...]).astype(BF)
    value = merged_ref[4, :, HS:]
    for head in range(4):
        lanes = slice(head % 2 * HS, head % 2 * HS + HS)
        query = merged_ref[2 * core + head // 2, :, lanes].astype(F32)
        query = norm(query, q_gain_ref[...]).astype(BF)
        scores = lax.dot_general(
            query, key, (((1,), (1,)), ((), ())), preferred_element_type=F32
        ) / math.sqrt(HS)
        scores = jnp.where(allowed, scores, -1e30)
        expo = jnp.exp(scores - jnp.max(scores, axis=-1, keepdims=True))
        weights = (expo / jnp.sum(expo, axis=-1, keepdims=True)).astype(BF)
        result[:, head * HS : (head + 1) * HS] = matmul(weights, value).astype(BF)

    padded, wide = slots.shape[1:]

    def slot_copy(o, source):
        columns = pl.ds(pl.multiple_of(source * wide, wide), wide)
        return pltpu.make_async_remote_copy(
            slots.at[o], out_ref.at[:, columns], slot_send.at[o], slot_recv.at[source],
            device_id={"tensor": o, "dp": y}, device_id_type=MESH,
        )

    source = 2 * z + core
    which = lax.broadcasted_iota(jnp.int32, (padded, rows), 0)

    def send(i, _):
        o = (chip + 1 + i) % 8
        hit = (which + o * capacity == slot) & (which < capacity)
        slots[o] = matmul(jnp.where(hit, 1.0, 0.0).astype(BF), result[...]).astype(BF)
        local = (o == chip) & (core == y)

        @pl.when(local)
        def _():
            out_ref[:, pl.ds(pl.multiple_of(source * wide, wide), wide)] = slots[o]

        @pl.when(jnp.logical_not(local))
        def _():
            slot_copy(o, source).start()

        return 0

    lax.fori_loop(0, 8, send, 0)

    def close(i, _):
        @pl.when(jnp.logical_not((i == chip) & (core == y)))
        def _():
            slot_copy(i, source).wait_send()

        @pl.when(jnp.logical_not((i == source) & (core == y)))
        def _():
            slot_copy(chip, i).wait_recv()

        return 0

    lax.fori_loop(0, 8, close, 0)


def whole_kernel(
    hidden_ref, down_ref, residual_ref, early_ref, middle_ref, merge_ref,
    q_gain_ref, k_gain_ref, length_ref, offset_ref, owner_ref, mask_ref,
    out_ref,
    taps, merged, tab, result, slots,
    hidden, weight, res, yout, own, yin, zin,
    w_sem, in_sem, far_send, far_recv, y_send, y_recv, z_send, z_recv, out_send, out_recv,
    weight2, yout2, own2, yin2, zin2,
    w_sem2, y_send2, y_recv2, z_send2, z_recv2, out_send2, out_recv2,
    slot_send, slot_recv,
):
    n_seq = length_ref.shape[1]
    capacity = residual_ref.shape[0] // 4 - 2

    def warm_up():
        copies = join_fetch(
            0, merge_ref.shape[2] // TILE, lax.axis_index("dp"), merge_ref, weight2, w_sem2
        )
        for copy in copies:
            copy.start()
        tab[0] = jnp.zeros(tab.shape[1:], jnp.int32)
        tab[0, 0:1, :n_seq] = length_ref[...]
        tab[0, 1:2, :n_seq] = offset_ref[...]
        tab[0, 2:3, :n_seq] = owner_ref[...]
        tab[0, 3:4] = mask_ref[...]

    down_part(
        (hidden_ref, down_ref, residual_ref, early_ref, middle_ref), taps,
        hidden, weight, res, tab, yout, own, yin, zin,
        w_sem, in_sem, far_send, far_recv, y_send, y_recv, z_send, z_recv, out_send, out_recv, warm_up,
    )
    join_part(
        taps, merge_ref, merged, weight2, yout2, own2, yin2, zin2,
        w_sem2, y_send2, y_recv2, z_send2, z_recv2, out_send2, out_recv2,
    )
    attend_part(
        merged, tab, q_gain_ref, k_gain_ref, out_ref, result, slots, slot_send, slot_recv,
        n_seq, capacity,
    )


def units(count, rows):
    shape = (rows, TILE)
    return [
        pltpu.VMEM((count, *shape), BF),
        pltpu.VMEM((count, *shape), BF),
        pltpu.VMEM((count, *shape), BF),
        pltpu.VMEM((2, count, *shape), BF),
    ]


def dma(*shape):
    return pltpu.SemaphoreType.DMA(shape)


def unit_sems(count):
    return [dma(count), dma(count), dma(count), dma(2, count)]


def grid_local(
    hidden_act,
    down_weight,
    residual,
    tap_early,
    tap_middle,
    merge_weight,
    q_gain,
    k_gain,
    lengths,
    offsets,
    owner_map,
    loss_mask,
):
    rows, depth = hidden_act.shape
    width = residual.shape[1]
    count = 4 * width // TILE
    parts, features, wide = merge_weight.shape
    count2 = wide // TILE
    capacity = rows // 4 - 2
    padded = -(-capacity // 16) * 16
    out = pl.pallas_call(
        whole_kernel,
        out_shape=jax.ShapeDtypeStruct((padded, QH * HS), BF),
        in_specs=[pl.BlockSpec(memory_space=pl.ANY)] * 6 + [pl.BlockSpec(memory_space=pltpu.VMEM)] * 6,
        out_specs=pl.BlockSpec(memory_space=pltpu.VMEM),
        scratch_shapes=[
            pltpu.VMEM((3, 2 * rows, width), BF),
            pltpu.VMEM((5, rows, TILE), BF),
            pltpu.VMEM((2, 8, rows), jnp.int32),
            pltpu.VMEM((rows, 4 * HS), BF),
            pltpu.VMEM((8, padded, 4 * HS), BF),
            pltpu.VMEM((2, rows, depth), BF),
            pltpu.VMEM((2, depth, TILE), BF),
            pltpu.VMEM((2, rows, width), BF),
            *units(count, rows),
            dma(2), dma(4), dma(5), dma(5),
            *unit_sems(count),
            dma(count // 2), dma(count // 2),
            pltpu.VMEM((2, parts, features, TILE), BF),
            *units(count2, rows),
            dma(2, 2),
            *unit_sems(count2),
            dma(count2), dma(count2),
            dma(8), dma(8),
        ],
        compiler_params=pltpu.CompilerParams(
            collective_id=0, has_side_effects=True, vmem_limit_bytes=60 << 20
        ),
        cost_estimate=pl.CostEstimate(
            flops=4 * rows * (depth * down_weight.shape[1] + parts * features * wide),
            bytes_accessed=4 * (down_weight.size + merge_weight.size),
            transcendentals=0,
        ),
        name="whole",
    )(
        hidden_act, down_weight, residual, tap_early, tap_middle, merge_weight,
        q_gain.reshape(1, HS), k_gain.reshape(1, HS), lengths, offsets, owner_map,
        loss_mask.reshape(1, rows),
    )
    return out[:capacity]


def plain_sums(hidden_act, down_weight, residual, tap_early, tap_middle, merge_weight):
    rows = hidden_act.shape[0]
    chips = lax.axis_size("tensor")
    core = lax.axis_index("dp")
    per_core = QH // chips
    wide = (per_core + 1) * HS
    hidden = lax.all_gather(hidden_act, "dp", axis=0, tiled=True)
    taps = lax.all_gather(jnp.concatenate([tap_early, tap_middle], axis=1), "dp", axis=0, tiled=True)
    partial_sum = jnp.dot(hidden, down_weight, preferred_element_type=F32).astype(BF)
    partial_sum = lax.all_to_all(partial_sum, "dp", split_axis=0, concat_axis=1, tiled=True)
    summed = lax.psum_scatter(partial_sum, "tensor", scatter_dimension=1, tiled=True).astype(F32)
    tap_late = (residual.astype(F32) + summed).astype(BF)
    late = lax.all_gather(tap_late, "dp", axis=0, tiled=True)

    weight = own_columns(merge_weight, core, per_core)
    joined = jnp.dot(taps, weight[:2].reshape(-1, weight.shape[2]), preferred_element_type=F32)
    joined = (joined + jnp.dot(late, weight[2], preferred_element_type=F32)).astype(BF)
    joined = joined.reshape(2, rows, chips // 2, wide).transpose(2, 0, 1, 3)
    merged = lax.psum_scatter(
        joined.reshape(chips, rows, wide), "tensor", scatter_dimension=0, tiled=False
    )
    query, mine_kv = merged[:, : per_core * HS], merged[:, per_core * HS :]
    other_kv = swap(mine_kv)
    key = jnp.where(core == 0, mine_kv, other_kv)
    value = jnp.where(core == 0, other_kv, mine_kv)
    return query, key, value


def local(
    hidden_act,
    down_weight,
    residual,
    tap_early,
    tap_middle,
    merge_weight,
    q_gain,
    k_gain,
    lengths,
    offsets,
    owner_map,
    loss_mask,
):
    rows = hidden_act.shape[0]
    chips = lax.axis_size("tensor")
    capacity = 2 * rows // chips - 2
    core = lax.axis_index("dp")
    chip = lax.axis_index("tensor")
    per_core = QH // chips
    n_seq = lengths.shape[1]

    table = jnp.concatenate([lengths[0], offsets[0], owner_map[0], loss_mask])
    tables = lax.all_gather(table, "dp", axis=0, tiled=False)
    query, key, value = plain_sums(hidden_act, down_weight, residual, tap_early, tap_middle, merge_weight)

    row = chip % 2
    mine = jnp.where(row == 0, tables[0], tables[1])
    length, offset, owner = [mine[i * n_seq : (i + 1) * n_seq] for i in range(3)]
    keep = (mine[3 * n_seq :] == 1).astype(F32)
    token = jnp.arange(rows, dtype=jnp.int32)
    inside = (offset[None, :] <= token[:, None]) & (token[:, None] < (offset + length)[None, :])
    sequence = jnp.sum(jnp.where(inside, jnp.arange(n_seq, dtype=jnp.int32)[None, :], 0), axis=1)
    index = jnp.arange(n_seq, dtype=jnp.int32)
    earlier = (owner[None, :] == owner[:, None]) & (index[None, :] < index[:, None])
    base = jnp.sum(jnp.where(earlier, length[None, :], 0), axis=1)
    start = owner * capacity + base - offset
    slot = token + jnp.sum(jnp.where(inside, start[None, :], 0), axis=1)
    place = (jnp.arange(chips * capacity, dtype=jnp.int32)[:, None] == slot[None, :]).astype(BF)

    result = attend(query, key, value, sequence, keep, q_gain, k_gain)
    slots = jnp.dot(place, result, preferred_element_type=F32).astype(BF)
    slots = lax.all_to_all(
        slots.reshape(chips, capacity, per_core * HS), "tensor", split_axis=0, concat_axis=0, tiled=True
    )
    slots = slots.reshape(chips // 2, 2, capacity, per_core * HS)
    first, second = slots[:, 0], slots[:, 1]
    own = jnp.where(core == 0, first, second)
    came = swap(jnp.where(core == 0, second, first))
    low = jnp.where(core == 0, own, came)
    high = jnp.where(core == 0, came, own)
    out = jnp.stack([low, high], axis=1)
    return out.transpose(2, 0, 1, 3).reshape(capacity, QH * HS)


def solution(mesh):
    shape = mesh.shape
    grid = shape["tensor"] == 8 and shape["dp"] == 2
    return jax.shard_map(
        grid_local if grid else local,
        mesh=mesh,
        in_specs=(
            P(("groups", "dp"), "tensor"),
            P("tensor", "dp"),
            P(("groups", "dp"), "tensor"),
            P(("groups", "dp"), "tensor"),
            P(("groups", "dp"), "tensor"),
            P(None, "tensor", "dp"),
            P(),
            P(),
            P(("groups", "dp"), None),
            P(("groups", "dp"), None),
            P(("groups", "dp"), None),
            P(("groups", "dp")),
        ),
        out_specs=P(("groups", "tensor", "dp"), None),
        check_vma=False,
    )
```

```python
import math

import jax
import jax.numpy as jnp
from jax import lax
from jax.experimental import pallas as pl
from jax.experimental.pallas import tpu as pltpu
from jax.sharding import PartitionSpec as P

QH = 32
KH = 4
HS = 128
BF = jnp.bfloat16
F32 = jnp.float32
MESH = pl.DeviceIdType.MESH


def swap(x):
    return lax.ppermute(x, "dp", [(0, 1), (1, 0)])


def head_order(per_core, core):
    order = []
    group = QH // KH
    for k in range(KH):
        for g in range(group // (2 * per_core)):
            first = k * group + g * 2 * per_core + core * per_core
            order += list(range(first, first + per_core))
            order.append(QH + core * KH + k)
    return order


def columns(x, blocks):
    return jnp.concatenate([x[..., b * HS : (b + 1) * HS] for b in blocks], axis=-1)


def own_columns(weight, core, per_core):
    half = weight.shape[-1] // HS
    need = [sorted(set(head_order(per_core, c))) for c in (0, 1)]
    send = [[b - c * half for b in need[1 - c] if b // half == c] for c in (0, 1)]
    sent = jnp.where(core == 0, columns(weight, send[0]), columns(weight, send[1]))
    came = swap(sent)
    both = jnp.concatenate([weight, came], axis=-1)

    def arranged(c):
        place = {b: b - c * half for b in need[c] if b // half == c}
        place.update({b + (1 - c) * half: half + i for i, b in enumerate(send[1 - c])})
        return columns(both, [place[b] for b in head_order(per_core, c)])

    return jnp.where(core == 0, arranged(0), arranged(1))


def norm(x, gain):
    return x * lax.rsqrt(jnp.mean(x * x, axis=-1, keepdims=True) + 1e-06) * gain


def attend(query, key, value, sequence, keep, q_gain, k_gain):
    tokens, wide = query.shape
    query = norm(query.astype(F32).reshape(tokens, wide // HS, HS), q_gain)
    key = norm(key.astype(F32), k_gain)
    scores = jnp.einsum("qhd,sd->hqs", query, key) / math.sqrt(HS)
    place = jnp.arange(tokens, dtype=jnp.int32)
    allowed = (sequence[:, None] == sequence[None, :]) & (place[None, :] <= place[:, None])
    scores = jnp.where(allowed, scores, -1e30)
    expo = jnp.exp(scores - jnp.max(scores, axis=-1, keepdims=True))
    weights = (expo / jnp.sum(expo, axis=-1, keepdims=True)).astype(BF)
    result = jnp.einsum("hqs,sd->qhd", weights, value, preferred_element_type=F32)
    return (result.reshape(tokens, wide) * keep[:, None]).astype(BF)


TILE = 256


def matmul(a, b):
    return jnp.dot(a, b, preferred_element_type=F32)


def greet(me):
    barrier = pltpu.get_barrier_semaphore()

    def signal(i, _):
        peer = (me + i) % 16
        pl.semaphore_signal(
            barrier, 1, device_id={"tensor": peer // 2, "dp": peer % 2}, device_id_type=MESH
        )
        return 0

    lax.fori_loop(1, 16, signal, 0)
    pl.semaphore_wait(barrier, 15)


AHEAD = 3


class Reduction:
    def __init__(self, count, z, y, dest, product, finish, buffers, sems):
        self.count, self.z, self.y, self.dest = count, z, y, dest
        self.product, self.finish = product, finish
        self.yout, self.own, self.yin, self.zin = buffers
        self.y_send, self.y_recv, self.z_send, self.z_recv = sems

    def y_copy(self, u):
        return pltpu.make_async_remote_copy(
            self.yout.at[u], self.yin.at[u], self.y_send.at[u], self.y_recv.at[u],
            device_id={"tensor": self.z * 2 + 1 - self.y}, device_id_type=MESH,
        )

    def z_copy(self, u, way):
        target = (self.z + 1 + 2 * way) % 4
        return pltpu.make_async_remote_copy(
            self.own.at[u], self.zin.at[way, u], self.z_send.at[u], self.z_recv.at[way, u],
            device_id={"tensor": target * 2 + self.y}, device_id_type=MESH,
        )

    def first(self, u):
        self.yout[u] = self.product(u, 0).astype(BF)

        @pl.when(u >= AHEAD)
        def _():
            self.y_copy(u - AHEAD).wait_send()

        self.y_copy(u).start()

    def second(self, u):
        self.own[u] = self.product(u, 1).astype(BF)

    def pair(self, u):
        return self.own[u].astype(F32) + self.yin[u].astype(F32)

    def pass_on(self, u, way, edge):
        z, own, zin = self.z, self.own, self.zin

        @pl.when((u >= 0) & (u < self.count))
        def _():
            ahead = self.dest(u) - z if way == 0 else z - self.dest(u)

            @pl.when(ahead > 0)
            def _():
                self.y_copy(u).wait_recv()

                @pl.when(z == edge)
                def _():
                    own[u] = self.pair(u).astype(BF)

                @pl.when(z != edge)
                def _():
                    self.z_copy(u, way).wait_recv()
                    own[u] = (self.pair(u) + zin[way, u].astype(F32)).astype(BF)

                self.z_copy(u, way).start()

    def chains(self, i):
        z, zin = self.z, self.zin
        self.pass_on(i - z, 0, 0)
        self.pass_on(i - 3 + z, 1, 3)
        u = i - 3

        @pl.when((u >= 0) & (u < self.count))
        def _():
            @pl.when(self.dest(u) == z)
            def _():
                self.y_copy(u).wait_recv()

                @pl.when(z == 0)
                def _():
                    self.z_copy(u, 1).wait_recv()
                    self.finish(u, self.pair(u) + zin[1, u].astype(F32))

                @pl.when(z == 3)
                def _():
                    self.z_copy(u, 0).wait_recv()
                    self.finish(u, self.pair(u) + zin[0, u].astype(F32))

                @pl.when((z > 0) & (z < 3))
                def _():
                    self.z_copy(u, 0).wait_recv()
                    self.z_copy(u, 1).wait_recv()
                    self.finish(u, self.pair(u) + zin[0, u].astype(F32) + zin[1, u].astype(F32))

    def close(self):
        for u in range(self.count - AHEAD, self.count):
            self.y_copy(u).wait_send()

        def last(u, _):
            @pl.when(self.dest(u) != self.z)
            def _():
                self.z_copy(u, 0).wait_send()

            return 0

        lax.fori_loop(0, self.count, last, 0)


def sums_part(
    ins, merge_ref, taps_ref, merged_ref, tab, fill_tab,
    hidden, weight, res, yout, own, yin, zin,
    w_sem, in_sem, far_send, far_recv, y_send, y_recv, z_send, z_recv, out_send, out_recv,
    weight2, yout2, own2, yin2, zin2,
    w_sem2, y_send2, y_recv2, z_send2, z_recv2, out_send2, out_recv2,
):
    hidden_ref, weight_ref, residual_ref, early_ref, middle_ref = ins
    rows, width = residual_ref.shape
    tiles = width // TILE
    count = 4 * tiles
    half_count = count // 2
    chip, core = lax.axis_index("tensor"), lax.axis_index("dp")
    z, y = chip // 2, chip % 2
    other = {"dp": 1 - core}
    mine = pl.ds(pl.multiple_of(core * rows, rows), rows)

    def fetch(s):
        u, stage = s // 2, s % 2
        block = 2 * (u % 2) + (1 - y) * (1 - stage) + y * stage
        column = block * width + (u // 2) % tiles * TILE
        source = weight_ref.at[:, pl.ds(pl.multiple_of(column, TILE), TILE)]
        return pltpu.make_async_copy(source, weight.at[s % 2], w_sem.at[s % 2])

    near = [
        pltpu.make_async_copy(hidden_ref, hidden.at[0], in_sem.at[0]),
        pltpu.make_async_copy(residual_ref, res.at[0], in_sem.at[1]),
        pltpu.make_async_copy(early_ref, taps_ref.at[0, mine], in_sem.at[2]),
        pltpu.make_async_copy(middle_ref, taps_ref.at[1, mine], in_sem.at[3]),
    ]
    near[0].start()
    fetch(0).start()
    fill_tab()
    greet(chip * 2 + core)
    pairs = [
        (hidden_ref, hidden.at[1]),
        (residual_ref, res.at[1]),
        (early_ref, taps_ref.at[0, mine]),
        (middle_ref, taps_ref.at[1, mine]),
        (tab.at[0], tab.at[1]),
    ]
    far = [
        pltpu.make_async_remote_copy(
            a, b, far_send.at[i], far_recv.at[i], device_id=other, device_id_type=MESH
        )
        for i, (a, b) in enumerate(pairs)
    ]
    far[0].start()
    for copy in near[1:]:
        copy.start()
    near[0].wait()
    for copy in far[1:]:
        copy.start()

    def half_of(u, stage):
        return (y + stage + u // half_count) % 2

    def product(u, stage):
        s = 2 * u + stage
        late_core = core == y if stage else core != y

        @pl.when((u == 0) & late_core)
        def _():
            far[0].wait_recv()

        fetch(s).wait()

        @pl.when(s + 1 < 2 * count)
        def _():
            fetch(s + 1).start()

        return matmul(hidden[(half_of(u, stage) + core) % 2], weight[s % 2])

    def late_place(u):
        return (
            2,
            pl.ds(pl.multiple_of(half_of(u, 1) * rows, rows), rows),
            pl.ds(pl.multiple_of((u // 2) % tiles * TILE, TILE), TILE),
        )

    def late_copy(u):
        place = taps_ref.at[late_place(u)]
        return pltpu.make_async_remote_copy(
            place, place, out_send.at[u // 2], out_recv.at[u // 2], device_id=other, device_id_type=MESH
        )

    def finish(u, total):
        column = pl.ds(pl.multiple_of((u // 2) % tiles * TILE, TILE), TILE)
        late = total + res[(half_of(u, 1) + core) % 2, :, column].astype(F32)
        taps_ref[late_place(u)] = late.astype(BF)
        late_copy(u).start()

    def late_arrived(start):
        @pl.when(z // 2 != core)
        def _():
            for r in range(start, start + tiles):
                late_copy(2 * r).wait_recv()

    down = Reduction(
        count, z, y, lambda u: 2 * core + u % 2, product, finish,
        (yout, own, yin, zin), (y_send, y_recv, z_send, z_recv),
    )

    count2 = merge_ref.shape[2] // TILE
    early = 3 + AHEAD

    def dest2(u, c):
        high = jnp.where(u < 2, 2, jnp.where(u < 6, 3, u - 6))
        return jnp.where(c == 0, u // 4, high)

    def spot(u, c):
        high = jnp.where(u < 2, u + 2, jnp.where(u < 6, u - 2, 4))
        return jnp.where(c == 0, u % 4, high)

    both = 2 * (count2 - early)

    def turn(u, stage):
        if stage:
            return jnp.where(u < count2 - early, early + 2 * u + 1, count2 + u)
        return jnp.where(u < early, u, early + 2 * (u - early))

    def fetch2(n):
        m = n - early
        turns = jnp.where(m % 2 == 0, early + m // 2, m // 2)
        u = jnp.where(m < 0, n, jnp.where(m < both, turns, n - count2))
        pair = (core == 1) & (u >= 6)
        parts = (jnp.where(pair, u + 6, 2 * u), jnp.where(pair, u + 10, 2 * u + 1))
        return [
            pltpu.make_async_copy(
                merge_ref.at[:, :, pl.ds(pl.multiple_of(part * HS, HS), HS)],
                weight2.at[n % 2, :, :, pl.ds(i * HS, HS)],
                w_sem2.at[n % 2, i],
            )
            for i, part in enumerate(parts)
        ]

    def product2(u, stage):
        n = turn(u, stage)
        for copy in fetch2(n):
            copy.wait()

        @pl.when(n + 1 < 2 * count2)
        def _():
            for copy in fetch2(n + 1):
                copy.start()

        row = y if stage else 1 - y
        part = pl.ds(pl.multiple_of(row * rows, rows), rows)
        total = matmul(taps_ref[0, part], weight2[n % 2, 0])
        total += matmul(taps_ref[1, part], weight2[n % 2, 1])
        return total + matmul(taps_ref[2, part], weight2[n % 2, 2])

    def merged_copy(u, c):
        place = merged_ref.at[spot(u, c)]
        return pltpu.make_async_remote_copy(
            place, place, out_send2.at[u], out_recv2.at[u], device_id=other, device_id_type=MESH
        )

    def finish2(u, total):
        merged_ref[spot(u, core)] = total.astype(BF)
        merged_copy(u, core).start()

    join = Reduction(
        count2, z, y, lambda u: dest2(u, core), product2, finish2,
        (yout2, own2, yin2, zin2), (y_send2, y_recv2, z_send2, z_recv2),
    )

    near[1].wait()
    far[1].wait_recv()
    for copy in fetch2(0):
        copy.start()

    def down_step(i, _):
        down.first(i)
        down.second(i)
        down.chains(i - AHEAD)
        return 0

    lax.fori_loop(0, count, down_step, 0)
    for copy in near[2:]:
        copy.wait()
    for copy in far:
        copy.wait_send()
    for copy in far[2:]:
        copy.wait_recv()
    late_arrived(0)

    def end_step(i, _):
        join.first(i)
        down.chains(count + i - AHEAD)
        return 0

    lax.fori_loop(0, early, end_step, 0)
    down.close()
    late_arrived(tiles)

    @pl.when(z // 2 == core)
    def _():
        for r in range(2 * tiles):
            late_copy(2 * r).wait_send()

    def join_step(j, _):
        @pl.when(j + early < count2)
        def _():
            join.first(j + early)

        @pl.when(j < count2)
        def _():
            join.second(j)

        join.chains(j)
        return 0

    lax.fori_loop(0, count2 + 3, join_step, 0)
    join.close()

    def close(u, _):
        @pl.when(dest2(u, core) == z)
        def _():
            merged_copy(u, core).wait_send()

        @pl.when(dest2(u, 1 - core) == z)
        def _():
            merged_copy(u, 1 - core).wait_recv()

        return 0

    lax.fori_loop(0, count2, close, 0)


def attend_part(
    merged_ref, tab, q_gain_ref, k_gain_ref, out_ref, result, slots, slot_send, slot_recv, n_seq, capacity
):
    rows = merged_ref.shape[1]
    chip, core = lax.axis_index("tensor"), lax.axis_index("dp")
    z, y = chip // 2, chip % 2
    table = tab[(core + y) % 2]
    length, offset, owner = [table[i : i + 1, :n_seq] for i in range(3)]
    keep = table[3:4]
    across = lax.broadcasted_iota(jnp.int32, (n_seq, n_seq), 1)
    down = lax.broadcasted_iota(jnp.int32, (n_seq, n_seq), 0)

    def upright(x):
        return jnp.sum(jnp.where(across == down, x, 0), axis=1, keepdims=True)

    length_up, offset_up, owner_up = upright(length), upright(offset), upright(owner)
    earlier = (owner == owner_up) & (across < down)
    base_up = jnp.sum(jnp.where(earlier, length, 0), axis=1, keepdims=True)
    start_up = owner_up * capacity + base_up - offset_up
    token = lax.broadcasted_iota(jnp.int32, (n_seq, rows), 1)
    inside = (offset_up <= token) & (token < offset_up + length_up)
    index = lax.broadcasted_iota(jnp.int32, (n_seq, rows), 0)
    sequence = jnp.sum(jnp.where(inside, index, 0), axis=0, keepdims=True)
    slot = jnp.sum(jnp.where(inside, start_up + token, 0), axis=0, keepdims=True)
    slot = jnp.where(keep == 1, slot, -1)
    token_up = lax.broadcasted_iota(jnp.int32, (rows, n_seq), 0)
    inside_up = (offset <= token_up) & (token_up < offset + length)
    index_up = lax.broadcasted_iota(jnp.int32, (rows, n_seq), 1)
    sequence_up = jnp.sum(jnp.where(inside_up, index_up, 0), axis=1, keepdims=True)
    later = lax.broadcasted_iota(jnp.int32, (rows, rows), 0)
    place = lax.broadcasted_iota(jnp.int32, (rows, rows), 1)
    allowed = (sequence_up == sequence) & (place <= later)

    key = norm(merged_ref[4, :, :HS].astype(F32), k_gain_ref[...]).astype(BF)
    value = merged_ref[4, :, HS:]
    for head in range(4):
        lanes = slice(head % 2 * HS, head % 2 * HS + HS)
        query = merged_ref[2 * core + head // 2, :, lanes].astype(F32)
        query = norm(query, q_gain_ref[...]).astype(BF)
        scores = lax.dot_general(
            query, key, (((1,), (1,)), ((), ())), preferred_element_type=F32
        ) / math.sqrt(HS)
        scores = jnp.where(allowed, scores, -1e30)
        expo = jnp.exp(scores - jnp.max(scores, axis=-1, keepdims=True))
        weights = (expo / jnp.sum(expo, axis=-1, keepdims=True)).astype(BF)
        result[:, head * HS : (head + 1) * HS] = matmul(weights, value).astype(BF)

    padded, wide = slots.shape[1:]

    def slot_copy(o, source):
        columns = pl.ds(pl.multiple_of(source * wide, wide), wide)
        return pltpu.make_async_remote_copy(
            slots.at[o], out_ref.at[:, columns], slot_send.at[o], slot_recv.at[source],
            device_id={"tensor": o, "dp": y}, device_id_type=MESH,
        )

    source = 2 * z + core
    which = lax.broadcasted_iota(jnp.int32, (padded, rows), 0)

    def send(i, _):
        o = (chip + 1 + i) % 8
        hit = (which + o * capacity == slot) & (which < capacity)
        slots[o] = matmul(jnp.where(hit, 1.0, 0.0).astype(BF), result[...]).astype(BF)
        local = (o == chip) & (core == y)

        @pl.when(local)
        def _():
            out_ref[:, pl.ds(pl.multiple_of(source * wide, wide), wide)] = slots[o]

        @pl.when(jnp.logical_not(local))
        def _():
            slot_copy(o, source).start()

        return 0

    lax.fori_loop(0, 8, send, 0)

    def close(i, _):
        @pl.when(jnp.logical_not((i == chip) & (core == y)))
        def _():
            slot_copy(i, source).wait_send()

        @pl.when(jnp.logical_not((i == source) & (core == y)))
        def _():
            slot_copy(chip, i).wait_recv()

        return 0

    lax.fori_loop(0, 8, close, 0)


def whole_kernel(
    hidden_ref, down_ref, residual_ref, early_ref, middle_ref, merge_ref,
    q_gain_ref, k_gain_ref, length_ref, offset_ref, owner_ref, mask_ref,
    out_ref,
    taps, merged, tab, result, slots,
    hidden, weight, res, yout, own, yin, zin,
    w_sem, in_sem, far_send, far_recv, y_send, y_recv, z_send, z_recv, out_send, out_recv,
    weight2, yout2, own2, yin2, zin2,
    w_sem2, y_send2, y_recv2, z_send2, z_recv2, out_send2, out_recv2,
    slot_send, slot_recv,
):
    n_seq = length_ref.shape[1]
    capacity = residual_ref.shape[0] // 4 - 2

    def fill_tab():
        tab[0] = jnp.zeros(tab.shape[1:], jnp.int32)
        tab[0, 0:1, :n_seq] = length_ref[...]
        tab[0, 1:2, :n_seq] = offset_ref[...]
        tab[0, 2:3, :n_seq] = owner_ref[...]
        tab[0, 3:4] = mask_ref[...]

    sums_part(
        (hidden_ref, down_ref, residual_ref, early_ref, middle_ref), merge_ref, taps, merged, tab, fill_tab,
        hidden, weight, res, yout, own, yin, zin,
        w_sem, in_sem, far_send, far_recv, y_send, y_recv, z_send, z_recv, out_send, out_recv,
        weight2, yout2, own2, yin2, zin2,
        w_sem2, y_send2, y_recv2, z_send2, z_recv2, out_send2, out_recv2,
    )
    attend_part(
        merged, tab, q_gain_ref, k_gain_ref, out_ref, result, slots, slot_send, slot_recv,
        n_seq, capacity,
    )


def units(count, rows):
    shape = (rows, TILE)
    return [
        pltpu.VMEM((count, *shape), BF),
        pltpu.VMEM((count, *shape), BF),
        pltpu.VMEM((count, *shape), BF),
        pltpu.VMEM((2, count, *shape), BF),
    ]


def dma(*shape):
    return pltpu.SemaphoreType.DMA(shape)


def unit_sems(count):
    return [dma(count), dma(count), dma(count), dma(2, count)]


def grid_local(
    hidden_act,
    down_weight,
    residual,
    tap_early,
    tap_middle,
    merge_weight,
    q_gain,
    k_gain,
    lengths,
    offsets,
    owner_map,
    loss_mask,
):
    rows, depth = hidden_act.shape
    width = residual.shape[1]
    count = 4 * width // TILE
    parts, features, wide = merge_weight.shape
    count2 = wide // TILE
    capacity = rows // 4 - 2
    padded = -(-capacity // 16) * 16
    out = pl.pallas_call(
        whole_kernel,
        out_shape=jax.ShapeDtypeStruct((padded, QH * HS), BF),
        in_specs=[pl.BlockSpec(memory_space=pl.ANY)] * 6 + [pl.BlockSpec(memory_space=pltpu.VMEM)] * 6,
        out_specs=pl.BlockSpec(memory_space=pltpu.VMEM),
        scratch_shapes=[
            pltpu.VMEM((3, 2 * rows, width), BF),
            pltpu.VMEM((5, rows, TILE), BF),
            pltpu.VMEM((2, 8, rows), jnp.int32),
            pltpu.VMEM((rows, 4 * HS), BF),
            pltpu.VMEM((8, padded, 4 * HS), BF),
            pltpu.VMEM((2, rows, depth), BF),
            pltpu.VMEM((2, depth, TILE), BF),
            pltpu.VMEM((2, rows, width), BF),
            *units(count, rows),
            dma(2), dma(4), dma(5), dma(5),
            *unit_sems(count),
            dma(count // 2), dma(count // 2),
            pltpu.VMEM((2, parts, features, TILE), BF),
            *units(count2, rows),
            dma(2, 2),
            *unit_sems(count2),
            dma(count2), dma(count2),
            dma(8), dma(8),
        ],
        compiler_params=pltpu.CompilerParams(
            collective_id=0, has_side_effects=True, vmem_limit_bytes=60 << 20
        ),
        cost_estimate=pl.CostEstimate(
            flops=4 * rows * (depth * down_weight.shape[1] + parts * features * wide),
            bytes_accessed=4 * (down_weight.size + merge_weight.size),
            transcendentals=0,
        ),
        name="whole",
    )(
        hidden_act, down_weight, residual, tap_early, tap_middle, merge_weight,
        q_gain.reshape(1, HS), k_gain.reshape(1, HS), lengths, offsets, owner_map,
        loss_mask.reshape(1, rows),
    )
    return out[:capacity]


def plain_sums(hidden_act, down_weight, residual, tap_early, tap_middle, merge_weight):
    rows = hidden_act.shape[0]
    chips = lax.axis_size("tensor")
    core = lax.axis_index("dp")
    per_core = QH // chips
    wide = (per_core + 1) * HS
    hidden = lax.all_gather(hidden_act, "dp", axis=0, tiled=True)
    taps = lax.all_gather(jnp.concatenate([tap_early, tap_middle], axis=1), "dp", axis=0, tiled=True)
    partial_sum = jnp.dot(hidden, down_weight, preferred_element_type=F32).astype(BF)
    partial_sum = lax.all_to_all(partial_sum, "dp", split_axis=0, concat_axis=1, tiled=True)
    summed = lax.psum_scatter(partial_sum, "tensor", scatter_dimension=1, tiled=True).astype(F32)
    tap_late = (residual.astype(F32) + summed).astype(BF)
    late = lax.all_gather(tap_late, "dp", axis=0, tiled=True)

    weight = own_columns(merge_weight, core, per_core)
    joined = jnp.dot(taps, weight[:2].reshape(-1, weight.shape[2]), preferred_element_type=F32)
    joined = (joined + jnp.dot(late, weight[2], preferred_element_type=F32)).astype(BF)
    joined = joined.reshape(2, rows, chips // 2, wide).transpose(2, 0, 1, 3)
    merged = lax.psum_scatter(
        joined.reshape(chips, rows, wide), "tensor", scatter_dimension=0, tiled=False
    )
    query, mine_kv = merged[:, : per_core * HS], merged[:, per_core * HS :]
    other_kv = swap(mine_kv)
    key = jnp.where(core == 0, mine_kv, other_kv)
    value = jnp.where(core == 0, other_kv, mine_kv)
    return query, key, value


def local(
    hidden_act,
    down_weight,
    residual,
    tap_early,
    tap_middle,
    merge_weight,
    q_gain,
    k_gain,
    lengths,
    offsets,
    owner_map,
    loss_mask,
):
    rows = hidden_act.shape[0]
    chips = lax.axis_size("tensor")
    capacity = 2 * rows // chips - 2
    core = lax.axis_index("dp")
    chip = lax.axis_index("tensor")
    per_core = QH // chips
    n_seq = lengths.shape[1]

    table = jnp.concatenate([lengths[0], offsets[0], owner_map[0], loss_mask])
    tables = lax.all_gather(table, "dp", axis=0, tiled=False)
    query, key, value = plain_sums(hidden_act, down_weight, residual, tap_early, tap_middle, merge_weight)

    row = chip % 2
    mine = jnp.where(row == 0, tables[0], tables[1])
    length, offset, owner = [mine[i * n_seq : (i + 1) * n_seq] for i in range(3)]
    keep = (mine[3 * n_seq :] == 1).astype(F32)
    token = jnp.arange(rows, dtype=jnp.int32)
    inside = (offset[None, :] <= token[:, None]) & (token[:, None] < (offset + length)[None, :])
    sequence = jnp.sum(jnp.where(inside, jnp.arange(n_seq, dtype=jnp.int32)[None, :], 0), axis=1)
    index = jnp.arange(n_seq, dtype=jnp.int32)
    earlier = (owner[None, :] == owner[:, None]) & (index[None, :] < index[:, None])
    base = jnp.sum(jnp.where(earlier, length[None, :], 0), axis=1)
    start = owner * capacity + base - offset
    slot = token + jnp.sum(jnp.where(inside, start[None, :], 0), axis=1)
    place = (jnp.arange(chips * capacity, dtype=jnp.int32)[:, None] == slot[None, :]).astype(BF)

    result = attend(query, key, value, sequence, keep, q_gain, k_gain)
    slots = jnp.dot(place, result, preferred_element_type=F32).astype(BF)
    slots = lax.all_to_all(
        slots.reshape(chips, capacity, per_core * HS), "tensor", split_axis=0, concat_axis=0, tiled=True
    )
    slots = slots.reshape(chips // 2, 2, capacity, per_core * HS)
    first, second = slots[:, 0], slots[:, 1]
    own = jnp.where(core == 0, first, second)
    came = swap(jnp.where(core == 0, second, first))
    low = jnp.where(core == 0, own, came)
    high = jnp.where(core == 0, came, own)
    out = jnp.stack([low, high], axis=1)
    return out.transpose(2, 0, 1, 3).reshape(capacity, QH * HS)


def solution(mesh):
    shape = mesh.shape
    grid = shape["tensor"] == 8 and shape["dp"] == 2
    return jax.shard_map(
        grid_local if grid else local,
        mesh=mesh,
        in_specs=(
            P(("groups", "dp"), "tensor"),
            P("tensor", "dp"),
            P(("groups", "dp"), "tensor"),
            P(("groups", "dp"), "tensor"),
            P(("groups", "dp"), "tensor"),
            P(None, "tensor", "dp"),
            P(),
            P(),
            P(("groups", "dp"), None),
            P(("groups", "dp"), None),
            P(("groups", "dp"), None),
            P(("groups", "dp")),
        ),
        out_specs=P(("groups", "tensor", "dp"), None),
        check_vma=False,
    )
```

```python
import math

import jax
import jax.numpy as jnp
from jax import lax
from jax.experimental import pallas as pl
from jax.experimental.pallas import tpu as pltpu
from jax.sharding import PartitionSpec as P

QH = 32
KH = 4
HS = 128
BF = jnp.bfloat16
F32 = jnp.float32
MESH = pl.DeviceIdType.MESH


def swap(x):
    return lax.ppermute(x, "dp", [(0, 1), (1, 0)])


def head_order(per_core, core):
    order = []
    group = QH // KH
    for k in range(KH):
        for g in range(group // (2 * per_core)):
            first = k * group + g * 2 * per_core + core * per_core
            order += list(range(first, first + per_core))
            order.append(QH + core * KH + k)
    return order


def columns(x, blocks):
    return jnp.concatenate([x[..., b * HS : (b + 1) * HS] for b in blocks], axis=-1)


def own_columns(weight, core, per_core):
    half = weight.shape[-1] // HS
    need = [sorted(set(head_order(per_core, c))) for c in (0, 1)]
    send = [[b - c * half for b in need[1 - c] if b // half == c] for c in (0, 1)]
    sent = jnp.where(core == 0, columns(weight, send[0]), columns(weight, send[1]))
    came = swap(sent)
    both = jnp.concatenate([weight, came], axis=-1)

    def arranged(c):
        place = {b: b - c * half for b in need[c] if b // half == c}
        place.update({b + (1 - c) * half: half + i for i, b in enumerate(send[1 - c])})
        return columns(both, [place[b] for b in head_order(per_core, c)])

    return jnp.where(core == 0, arranged(0), arranged(1))


def norm(x, gain):
    return x * lax.rsqrt(jnp.mean(x * x, axis=-1, keepdims=True) + 1e-06) * gain


def attend(query, key, value, sequence, keep, q_gain, k_gain):
    tokens, wide = query.shape
    query = norm(query.astype(F32).reshape(tokens, wide // HS, HS), q_gain)
    key = norm(key.astype(F32), k_gain)
    scores = jnp.einsum("qhd,sd->hqs", query, key) / math.sqrt(HS)
    place = jnp.arange(tokens, dtype=jnp.int32)
    allowed = (sequence[:, None] == sequence[None, :]) & (place[None, :] <= place[:, None])
    scores = jnp.where(allowed, scores, -1e30)
    expo = jnp.exp(scores - jnp.max(scores, axis=-1, keepdims=True))
    weights = (expo / jnp.sum(expo, axis=-1, keepdims=True)).astype(BF)
    result = jnp.einsum("hqs,sd->qhd", weights, value, preferred_element_type=F32)
    return (result.reshape(tokens, wide) * keep[:, None]).astype(BF)


TILE = 256


def matmul(a, b):
    return jnp.dot(a, b, preferred_element_type=F32)


def greet(me):
    barrier = pltpu.get_barrier_semaphore()

    def signal(i, _):
        peer = (me + i) % 16
        pl.semaphore_signal(
            barrier, 1, device_id={"tensor": peer // 2, "dp": peer % 2}, device_id_type=MESH
        )
        return 0

    lax.fori_loop(1, 16, signal, 0)
    pl.semaphore_wait(barrier, 15)


AHEAD = 4


class Reduction:
    def __init__(self, count, z, y, dest, product, finish, buffers, sems):
        self.count, self.z, self.y, self.dest = count, z, y, dest
        self.product, self.finish = product, finish
        self.yout, self.own, self.yin, self.zin = buffers
        self.y_send, self.y_recv, self.z_send, self.z_recv = sems

    def y_copy(self, u):
        return pltpu.make_async_remote_copy(
            self.yout.at[u], self.yin.at[u], self.y_send.at[u], self.y_recv.at[u],
            device_id={"tensor": self.z * 2 + 1 - self.y}, device_id_type=MESH,
        )

    def z_copy(self, u, way):
        target = (self.z + 1 + 2 * way) % 4
        return pltpu.make_async_remote_copy(
            self.own.at[u], self.zin.at[way, u], self.z_send.at[u], self.z_recv.at[way, u],
            device_id={"tensor": target * 2 + self.y}, device_id_type=MESH,
        )

    def first(self, u):
        self.yout[u] = self.product(u, 0).astype(BF)

        @pl.when(u >= AHEAD)
        def _():
            self.y_copy(u - AHEAD).wait_send()

        self.y_copy(u).start()

    def second(self, u):
        self.own[u] = self.product(u, 1).astype(BF)

    def pair(self, u):
        return self.own[u].astype(F32) + self.yin[u].astype(F32)

    def pass_on(self, u, way, edge):
        z, own, zin = self.z, self.own, self.zin

        @pl.when((u >= 0) & (u < self.count))
        def _():
            ahead = self.dest(u) - z if way == 0 else z - self.dest(u)

            @pl.when(ahead > 0)
            def _():
                self.y_copy(u).wait_recv()

                @pl.when(z == edge)
                def _():
                    own[u] = self.pair(u).astype(BF)

                @pl.when(z != edge)
                def _():
                    self.z_copy(u, way).wait_recv()
                    own[u] = (self.pair(u) + zin[way, u].astype(F32)).astype(BF)

                self.z_copy(u, way).start()

    def chains(self, i):
        z, zin = self.z, self.zin
        self.pass_on(i - z, 0, 0)
        self.pass_on(i - 3 + z, 1, 3)
        u = i - 3

        @pl.when((u >= 0) & (u < self.count))
        def _():
            @pl.when(self.dest(u) == z)
            def _():
                self.y_copy(u).wait_recv()

                @pl.when(z == 0)
                def _():
                    self.z_copy(u, 1).wait_recv()
                    self.finish(u, self.pair(u) + zin[1, u].astype(F32))

                @pl.when(z == 3)
                def _():
                    self.z_copy(u, 0).wait_recv()
                    self.finish(u, self.pair(u) + zin[0, u].astype(F32))

                @pl.when((z > 0) & (z < 3))
                def _():
                    self.z_copy(u, 0).wait_recv()
                    self.z_copy(u, 1).wait_recv()
                    self.finish(u, self.pair(u) + zin[0, u].astype(F32) + zin[1, u].astype(F32))

    def close(self):
        for u in range(self.count - AHEAD, self.count):
            self.y_copy(u).wait_send()

        def last(u, _):
            @pl.when(self.dest(u) != self.z)
            def _():
                self.z_copy(u, 0).wait_send()

            return 0

        lax.fori_loop(0, self.count, last, 0)


def sums_part(
    ins, merge_ref, taps_ref, merged_ref, tab, fill_tab,
    hidden, weight, res, yout, own, yin, zin,
    w_sem, in_sem, far_send, far_recv, y_send, y_recv, z_send, z_recv, out_send, out_recv,
    weight2, yout2, own2, yin2, zin2,
    w_sem2, y_send2, y_recv2, z_send2, z_recv2, out_send2, out_recv2,
):
    hidden_ref, weight_ref, residual_ref, early_ref, middle_ref = ins
    rows, width = residual_ref.shape
    tiles = width // TILE
    count = 4 * tiles
    half_count = count // 2
    chip, core = lax.axis_index("tensor"), lax.axis_index("dp")
    z, y = chip // 2, chip % 2
    other = {"dp": 1 - core}
    mine = pl.ds(pl.multiple_of(core * rows, rows), rows)

    def fetch(s):
        u, stage = s // 2, s % 2
        block = 2 * (u % 2) + (1 - y) * (1 - stage) + y * stage
        column = block * width + (u // 2) % tiles * TILE
        source = weight_ref.at[:, pl.ds(pl.multiple_of(column, TILE), TILE)]
        return pltpu.make_async_copy(source, weight.at[s % 2], w_sem.at[s % 2])

    near = [
        pltpu.make_async_copy(hidden_ref, hidden.at[0], in_sem.at[0]),
        pltpu.make_async_copy(residual_ref, res.at[0], in_sem.at[1]),
        pltpu.make_async_copy(early_ref, taps_ref.at[0, mine], in_sem.at[2]),
        pltpu.make_async_copy(middle_ref, taps_ref.at[1, mine], in_sem.at[3]),
    ]
    near[0].start()
    fetch(0).start()
    fill_tab()
    greet(chip * 2 + core)
    pairs = [
        (hidden_ref, hidden.at[1]),
        (residual_ref, res.at[1]),
        (early_ref, taps_ref.at[0, mine]),
        (middle_ref, taps_ref.at[1, mine]),
        (tab.at[0], tab.at[1]),
    ]
    far = [
        pltpu.make_async_remote_copy(
            a, b, far_send.at[i], far_recv.at[i], device_id=other, device_id_type=MESH
        )
        for i, (a, b) in enumerate(pairs)
    ]
    far[0].start()
    for copy in near[1:]:
        copy.start()
    near[0].wait()
    for copy in far[1:]:
        copy.start()

    def half_of(u, stage):
        return (y + stage + u // half_count) % 2

    def product(u, stage):
        s = 2 * u + stage
        late_core = core == y if stage else core != y

        @pl.when((u == 0) & late_core)
        def _():
            far[0].wait_recv()

        fetch(s).wait()

        @pl.when(s + 1 < 2 * count)
        def _():
            fetch(s + 1).start()

        return matmul(hidden[(half_of(u, stage) + core) % 2], weight[s % 2])

    def late_place(u):
        return (
            2,
            pl.ds(pl.multiple_of(half_of(u, 1) * rows, rows), rows),
            pl.ds(pl.multiple_of((u // 2) % tiles * TILE, TILE), TILE),
        )

    def late_copy(u):
        place = taps_ref.at[late_place(u)]
        return pltpu.make_async_remote_copy(
            place, place, out_send.at[u // 2], out_recv.at[u // 2], device_id=other, device_id_type=MESH
        )

    def finish(u, total):
        column = pl.ds(pl.multiple_of((u // 2) % tiles * TILE, TILE), TILE)
        late = total + res[(half_of(u, 1) + core) % 2, :, column].astype(F32)
        taps_ref[late_place(u)] = late.astype(BF)
        late_copy(u).start()

    def late_arrived(start):
        @pl.when(z // 2 != core)
        def _():
            for r in range(start, start + tiles):
                late_copy(2 * r).wait_recv()

    down = Reduction(
        count, z, y, lambda u: 2 * core + u % 2, product, finish,
        (yout, own, yin, zin), (y_send, y_recv, z_send, z_recv),
    )

    count2 = merge_ref.shape[2] // TILE
    early = 3 + AHEAD

    def dest2(u, c):
        high = jnp.where(u < 2, 2, jnp.where(u < 6, 3, u - 6))
        return jnp.where(c == 0, u // 4, high)

    def spot(u, c):
        high = jnp.where(u < 2, u + 2, jnp.where(u < 6, u - 2, 4))
        return jnp.where(c == 0, u % 4, high)

    both = 2 * (count2 - early)

    def turn(u, stage):
        if stage:
            return jnp.where(u < count2 - early, early + 2 * u + 1, count2 + u)
        return jnp.where(u < early, u, early + 2 * (u - early))

    def fetch2(n):
        m = n - early
        turns = jnp.where(m % 2 == 0, early + m // 2, m // 2)
        u = jnp.where(m < 0, n, jnp.where(m < both, turns, n - count2))
        pair = (core == 1) & (u >= 6)
        parts = (jnp.where(pair, u + 6, 2 * u), jnp.where(pair, u + 10, 2 * u + 1))
        return [
            pltpu.make_async_copy(
                merge_ref.at[:, :, pl.ds(pl.multiple_of(part * HS, HS), HS)],
                weight2.at[n % 2, :, :, pl.ds(i * HS, HS)],
                w_sem2.at[n % 2, i],
            )
            for i, part in enumerate(parts)
        ]

    def product2(u, stage):
        n = turn(u, stage)
        for copy in fetch2(n):
            copy.wait()

        @pl.when(n + 1 < 2 * count2)
        def _():
            for copy in fetch2(n + 1):
                copy.start()

        row = y if stage else 1 - y
        part = pl.ds(pl.multiple_of(row * rows, rows), rows)
        total = matmul(taps_ref[0, part], weight2[n % 2, 0])
        total += matmul(taps_ref[1, part], weight2[n % 2, 1])
        return total + matmul(taps_ref[2, part], weight2[n % 2, 2])

    def merged_copy(u, c):
        place = merged_ref.at[spot(u, c)]
        return pltpu.make_async_remote_copy(
            place, place, out_send2.at[u], out_recv2.at[u], device_id=other, device_id_type=MESH
        )

    def finish2(u, total):
        merged_ref[spot(u, core)] = total.astype(BF)
        merged_copy(u, core).start()

    join = Reduction(
        count2, z, y, lambda u: dest2(u, core), product2, finish2,
        (yout2, own2, yin2, zin2), (y_send2, y_recv2, z_send2, z_recv2),
    )

    near[1].wait()
    far[1].wait_recv()
    for copy in fetch2(0):
        copy.start()

    def down_step(i, _):
        down.first(i)
        down.second(i)
        down.chains(i - AHEAD)
        return 0

    lax.fori_loop(0, count, down_step, 0)
    for copy in near[2:]:
        copy.wait()
    for copy in far:
        copy.wait_send()
    for copy in far[2:]:
        copy.wait_recv()
    late_arrived(0)

    def end_step(i, _):
        join.first(i)
        down.chains(count + i - AHEAD)
        return 0

    lax.fori_loop(0, early, end_step, 0)
    down.close()
    late_arrived(tiles)

    @pl.when(z // 2 == core)
    def _():
        for r in range(2 * tiles):
            late_copy(2 * r).wait_send()

    def join_step(j, _):
        @pl.when(j + early < count2)
        def _():
            join.first(j + early)

        @pl.when(j < count2)
        def _():
            join.second(j)

        join.chains(j)
        return 0

    lax.fori_loop(0, count2 + 3, join_step, 0)
    join.close()

    def close(u, _):
        @pl.when(dest2(u, core) == z)
        def _():
            merged_copy(u, core).wait_send()

        @pl.when(dest2(u, 1 - core) == z)
        def _():
            merged_copy(u, 1 - core).wait_recv()

        return 0

    lax.fori_loop(0, count2, close, 0)


def attend_part(
    merged_ref, tab, q_gain_ref, k_gain_ref, out_ref, result, slots, slot_send, slot_recv, n_seq, capacity
):
    rows = merged_ref.shape[1]
    chip, core = lax.axis_index("tensor"), lax.axis_index("dp")
    z, y = chip // 2, chip % 2
    table = tab[(core + y) % 2]
    length, offset, owner = [table[i : i + 1, :n_seq] for i in range(3)]
    keep = table[3:4]
    across = lax.broadcasted_iota(jnp.int32, (n_seq, n_seq), 1)
    down = lax.broadcasted_iota(jnp.int32, (n_seq, n_seq), 0)

    def upright(x):
        return jnp.sum(jnp.where(across == down, x, 0), axis=1, keepdims=True)

    length_up, offset_up, owner_up = upright(length), upright(offset), upright(owner)
    earlier = (owner == owner_up) & (across < down)
    base_up = jnp.sum(jnp.where(earlier, length, 0), axis=1, keepdims=True)
    start_up = owner_up * capacity + base_up - offset_up
    token = lax.broadcasted_iota(jnp.int32, (n_seq, rows), 1)
    inside = (offset_up <= token) & (token < offset_up + length_up)
    index = lax.broadcasted_iota(jnp.int32, (n_seq, rows), 0)
    sequence = jnp.sum(jnp.where(inside, index, 0), axis=0, keepdims=True)
    slot = jnp.sum(jnp.where(inside, start_up + token, 0), axis=0, keepdims=True)
    slot = jnp.where(keep == 1, slot, -1)
    token_up = lax.broadcasted_iota(jnp.int32, (rows, n_seq), 0)
    inside_up = (offset <= token_up) & (token_up < offset + length)
    index_up = lax.broadcasted_iota(jnp.int32, (rows, n_seq), 1)
    sequence_up = jnp.sum(jnp.where(inside_up, index_up, 0), axis=1, keepdims=True)
    later = lax.broadcasted_iota(jnp.int32, (rows, rows), 0)
    place = lax.broadcasted_iota(jnp.int32, (rows, rows), 1)
    allowed = (sequence_up == sequence) & (place <= later)

    key = norm(merged_ref[4, :, :HS].astype(F32), k_gain_ref[...]).astype(BF)
    value = merged_ref[4, :, HS:]
    padded, wide = slots.shape[2:]
    source = 2 * z + core
    which = lax.broadcasted_iota(jnp.int32, (padded, rows), 0)

    def slot_columns(part, place):
        return pl.ds(pl.multiple_of((2 * place + part) * wide, wide), wide)

    def slot_copy(part, o, place):
        return pltpu.make_async_remote_copy(
            slots.at[part, o], out_ref.at[:, slot_columns(part, place)],
            slot_send.at[part, o], slot_recv.at[part, place],
            device_id={"tensor": o, "dp": y}, device_id_type=MESH,
        )

    for part in range(2):
        for head in range(2):
            lanes = slice(head * HS, (head + 1) * HS)
            query = merged_ref[2 * core + part, :, lanes].astype(F32)
            query = norm(query, q_gain_ref[...]).astype(BF)
            scores = lax.dot_general(
                query, key, (((1,), (1,)), ((), ())), preferred_element_type=F32
            ) / math.sqrt(HS)
            scores = jnp.where(allowed, scores, -1e30)
            expo = jnp.exp(scores - jnp.max(scores, axis=-1, keepdims=True))
            weights = (expo / jnp.sum(expo, axis=-1, keepdims=True)).astype(BF)
            result[part, :, lanes] = matmul(weights, value).astype(BF)

        def send(i, _):
            o = (chip + 1 + i) % 8
            hit = (which + o * capacity == slot) & (which < capacity)
            hit = jnp.where(hit, 1.0, 0.0).astype(BF)
            slots[part, o] = matmul(hit, result[part]).astype(BF)
            local = (o == chip) & (core == y)

            @pl.when(local)
            def _():
                out_ref[:, slot_columns(part, source)] = slots[part, o]

            @pl.when(jnp.logical_not(local))
            def _():
                slot_copy(part, o, source).start()

            return 0

        lax.fori_loop(0, 8, send, 0)

    for part in range(2):

        def close(i, _):
            @pl.when(jnp.logical_not((i == chip) & (core == y)))
            def _():
                slot_copy(part, i, source).wait_send()

            @pl.when(jnp.logical_not((i == source) & (core == y)))
            def _():
                slot_copy(part, chip, i).wait_recv()

            return 0

        lax.fori_loop(0, 8, close, 0)


def whole_kernel(
    hidden_ref, down_ref, residual_ref, early_ref, middle_ref, merge_ref,
    q_gain_ref, k_gain_ref, length_ref, offset_ref, owner_ref, mask_ref,
    out_ref,
    taps, merged, tab, result, slots,
    hidden, weight, res, yout, own, yin, zin,
    w_sem, in_sem, far_send, far_recv, y_send, y_recv, z_send, z_recv, out_send, out_recv,
    weight2, yout2, own2, yin2, zin2,
    w_sem2, y_send2, y_recv2, z_send2, z_recv2, out_send2, out_recv2,
    slot_send, slot_recv,
):
    n_seq = length_ref.shape[1]
    capacity = residual_ref.shape[0] // 4 - 2

    def fill_tab():
        tab[0] = jnp.zeros(tab.shape[1:], jnp.int32)
        tab[0, 0:1, :n_seq] = length_ref[...]
        tab[0, 1:2, :n_seq] = offset_ref[...]
        tab[0, 2:3, :n_seq] = owner_ref[...]
        tab[0, 3:4] = mask_ref[...]

    sums_part(
        (hidden_ref, down_ref, residual_ref, early_ref, middle_ref), merge_ref, taps, merged, tab, fill_tab,
        hidden, weight, res, yout, own, yin, zin,
        w_sem, in_sem, far_send, far_recv, y_send, y_recv, z_send, z_recv, out_send, out_recv,
        weight2, yout2, own2, yin2, zin2,
        w_sem2, y_send2, y_recv2, z_send2, z_recv2, out_send2, out_recv2,
    )
    attend_part(
        merged, tab, q_gain_ref, k_gain_ref, out_ref, result, slots, slot_send, slot_recv,
        n_seq, capacity,
    )


def units(count, rows):
    shape = (rows, TILE)
    return [
        pltpu.VMEM((count, *shape), BF),
        pltpu.VMEM((count, *shape), BF),
        pltpu.VMEM((count, *shape), BF),
        pltpu.VMEM((2, count, *shape), BF),
    ]


def dma(*shape):
    return pltpu.SemaphoreType.DMA(shape)


def unit_sems(count):
    return [dma(count), dma(count), dma(count), dma(2, count)]


def grid_local(
    hidden_act,
    down_weight,
    residual,
    tap_early,
    tap_middle,
    merge_weight,
    q_gain,
    k_gain,
    lengths,
    offsets,
    owner_map,
    loss_mask,
):
    rows, depth = hidden_act.shape
    width = residual.shape[1]
    count = 4 * width // TILE
    parts, features, wide = merge_weight.shape
    count2 = wide // TILE
    capacity = rows // 4 - 2
    padded = -(-capacity // 16) * 16
    out = pl.pallas_call(
        whole_kernel,
        out_shape=jax.ShapeDtypeStruct((padded, QH * HS), BF),
        in_specs=[pl.BlockSpec(memory_space=pl.ANY)] * 6 + [pl.BlockSpec(memory_space=pltpu.VMEM)] * 6,
        out_specs=pl.BlockSpec(memory_space=pltpu.VMEM),
        scratch_shapes=[
            pltpu.VMEM((3, 2 * rows, width), BF),
            pltpu.VMEM((5, rows, TILE), BF),
            pltpu.VMEM((2, 8, rows), jnp.int32),
            pltpu.VMEM((2, rows, 2 * HS), BF),
            pltpu.VMEM((2, 8, padded, 2 * HS), BF),
            pltpu.VMEM((2, rows, depth), BF),
            pltpu.VMEM((2, depth, TILE), BF),
            pltpu.VMEM((2, rows, width), BF),
            *units(count, rows),
            dma(2), dma(4), dma(5), dma(5),
            *unit_sems(count),
            dma(count // 2), dma(count // 2),
            pltpu.VMEM((2, parts, features, TILE), BF),
            *units(count2, rows),
            dma(2, 2),
            *unit_sems(count2),
            dma(count2), dma(count2),
            dma(2, 8), dma(2, 8),
        ],
        compiler_params=pltpu.CompilerParams(
            collective_id=0, has_side_effects=True, vmem_limit_bytes=60 << 20
        ),
        cost_estimate=pl.CostEstimate(
            flops=4 * rows * (depth * down_weight.shape[1] + parts * features * wide),
            bytes_accessed=4 * (down_weight.size + merge_weight.size),
            transcendentals=0,
        ),
        name="whole",
    )(
        hidden_act, down_weight, residual, tap_early, tap_middle, merge_weight,
        q_gain.reshape(1, HS), k_gain.reshape(1, HS), lengths, offsets, owner_map,
        loss_mask.reshape(1, rows),
    )
    return out[:capacity]


def plain_sums(hidden_act, down_weight, residual, tap_early, tap_middle, merge_weight):
    rows = hidden_act.shape[0]
    chips = lax.axis_size("tensor")
    core = lax.axis_index("dp")
    per_core = QH // chips
    wide = (per_core + 1) * HS
    hidden = lax.all_gather(hidden_act, "dp", axis=0, tiled=True)
    taps = lax.all_gather(jnp.concatenate([tap_early, tap_middle], axis=1), "dp", axis=0, tiled=True)
    partial_sum = jnp.dot(hidden, down_weight, preferred_element_type=F32).astype(BF)
    partial_sum = lax.all_to_all(partial_sum, "dp", split_axis=0, concat_axis=1, tiled=True)
    summed = lax.psum_scatter(partial_sum, "tensor", scatter_dimension=1, tiled=True).astype(F32)
    tap_late = (residual.astype(F32) + summed).astype(BF)
    late = lax.all_gather(tap_late, "dp", axis=0, tiled=True)

    weight = own_columns(merge_weight, core, per_core)
    joined = jnp.dot(taps, weight[:2].reshape(-1, weight.shape[2]), preferred_element_type=F32)
    joined = (joined + jnp.dot(late, weight[2], preferred_element_type=F32)).astype(BF)
    joined = joined.reshape(2, rows, chips // 2, wide).transpose(2, 0, 1, 3)
    merged = lax.psum_scatter(
        joined.reshape(chips, rows, wide), "tensor", scatter_dimension=0, tiled=False
    )
    query, mine_kv = merged[:, : per_core * HS], merged[:, per_core * HS :]
    other_kv = swap(mine_kv)
    key = jnp.where(core == 0, mine_kv, other_kv)
    value = jnp.where(core == 0, other_kv, mine_kv)
    return query, key, value


def local(
    hidden_act,
    down_weight,
    residual,
    tap_early,
    tap_middle,
    merge_weight,
    q_gain,
    k_gain,
    lengths,
    offsets,
    owner_map,
    loss_mask,
):
    rows = hidden_act.shape[0]
    chips = lax.axis_size("tensor")
    capacity = 2 * rows // chips - 2
    core = lax.axis_index("dp")
    chip = lax.axis_index("tensor")
    per_core = QH // chips
    n_seq = lengths.shape[1]

    table = jnp.concatenate([lengths[0], offsets[0], owner_map[0], loss_mask])
    tables = lax.all_gather(table, "dp", axis=0, tiled=False)
    query, key, value = plain_sums(hidden_act, down_weight, residual, tap_early, tap_middle, merge_weight)

    row = chip % 2
    mine = jnp.where(row == 0, tables[0], tables[1])
    length, offset, owner = [mine[i * n_seq : (i + 1) * n_seq] for i in range(3)]
    keep = (mine[3 * n_seq :] == 1).astype(F32)
    token = jnp.arange(rows, dtype=jnp.int32)
    inside = (offset[None, :] <= token[:, None]) & (token[:, None] < (offset + length)[None, :])
    sequence = jnp.sum(jnp.where(inside, jnp.arange(n_seq, dtype=jnp.int32)[None, :], 0), axis=1)
    index = jnp.arange(n_seq, dtype=jnp.int32)
    earlier = (owner[None, :] == owner[:, None]) & (index[None, :] < index[:, None])
    base = jnp.sum(jnp.where(earlier, length[None, :], 0), axis=1)
    start = owner * capacity + base - offset
    slot = token + jnp.sum(jnp.where(inside, start[None, :], 0), axis=1)
    place = (jnp.arange(chips * capacity, dtype=jnp.int32)[:, None] == slot[None, :]).astype(BF)

    result = attend(query, key, value, sequence, keep, q_gain, k_gain)
    slots = jnp.dot(place, result, preferred_element_type=F32).astype(BF)
    slots = lax.all_to_all(
        slots.reshape(chips, capacity, per_core * HS), "tensor", split_axis=0, concat_axis=0, tiled=True
    )
    slots = slots.reshape(chips // 2, 2, capacity, per_core * HS)
    first, second = slots[:, 0], slots[:, 1]
    own = jnp.where(core == 0, first, second)
    came = swap(jnp.where(core == 0, second, first))
    low = jnp.where(core == 0, own, came)
    high = jnp.where(core == 0, came, own)
    out = jnp.stack([low, high], axis=1)
    return out.transpose(2, 0, 1, 3).reshape(capacity, QH * HS)


def solution(mesh):
    shape = mesh.shape
    grid = shape["tensor"] == 8 and shape["dp"] == 2
    return jax.shard_map(
        grid_local if grid else local,
        mesh=mesh,
        in_specs=(
            P(("groups", "dp"), "tensor"),
            P("tensor", "dp"),
            P(("groups", "dp"), "tensor"),
            P(("groups", "dp"), "tensor"),
            P(("groups", "dp"), "tensor"),
            P(None, "tensor", "dp"),
            P(),
            P(),
            P(("groups", "dp"), None),
            P(("groups", "dp"), None),
            P(("groups", "dp"), None),
            P(("groups", "dp")),
        ),
        out_specs=P(("groups", "tensor", "dp"), None),
        check_vma=False,
    )
```
